32 devices in a mesh: fix: 16 (over z, x, core), subj: 2 (over y).
Axes of the slice: x: 2, y: 2, z: 4, core: 2. Of those that a mesh axis runs over, the one named last changes fastest.
Arguments:
- fixels: float32 [16384, 256], P('fix', 'subj'), may hold values from -6 to 6
- conn_tiles: float32 [128, 4, 128, 128], P('fix'), may hold values from -0.25 to 0.25
- columns: int32 [128, 4], P('fix'), may hold values from 0 to 127, as said below
- nuisance: float32 [4, 256], P(None, 'subj'), may hold values from -5 to 5
- nuisance_pinv: float32 [4, 256], P(None, 'subj'), may hold values from -0.375 to 0.375
- contrast: float32 [4, 256], replicated, may hold values from -0.375 to 0.375
- perm_table: int32 [128, 256], P(None, 'subj'), may hold values from 0 to 255, each once within a row
Outputs:
- projections: float32 [512, 16384], P('subj', 'fix')
The draws below stay inside these ranges and needn't reach their ends.
Inputs may be any that keep to these rules, and one draw needn't show every extreme that they name: `columns`: device j of fix holds blocks j * 8 to (j + 1) * 8 - 1. The 32 entries of one device's rows name blocks of any one device at most 2 times, and in every draw some device's blocks are named exactly 2 times by the rows of every device. `perm_table`: each row is a permutation of the 256 subjects.
All inputs are finite; a program needn't handle non-finite values.
Results may differ from the reference program's by a relative error of at most 0.000071.
Values sent between devices are 32-bit elements; how exact they have to be, the bound alone decides.
No kernel may reach another device: no remote copies, remote signals or barrier semaphores. Data moves between devices by JAX's collectives and lax.ppermute only.
A program may use at most 64 MiB of HBM per device.

```python
import jax
import jax.numpy as jnp
from jax import lax

BS = 128
BLK_DEV = 8
TILES = 4
PERMS = 128
REGS = 4
NUIS = 4
SUBJ = 256
FIX_BLOCKS = 128
FIXELS = 16384
N_FIX = 16


def draw_columns(key, part):
    hub = jax.random.randint(jax.random.fold_in(key, 7777), (), 0, N_FIX)

    def one_device(device):
        dev_key = jax.random.fold_in(key, device)
        key_order, key_shuffle, key_local = jax.random.split(dev_key, 3)
        order = jax.random.permutation(key_order, N_FIX)
        where_hub = jnp.argmax(order == hub)
        first = order[0]
        order = order.at[where_hub].set(first).at[0].set(hub)
        positions = jnp.arange(BLK_DEV * TILES)
        owners = order[positions % N_FIX]
        owners = jax.random.permutation(key_shuffle, owners)
        local_index = jax.random.randint(key_local, (BLK_DEV * TILES,), 0, BLK_DEV)
        return (owners * BLK_DEV + local_index).reshape(BLK_DEV, TILES)
    result = jax.vmap(one_device)(jnp.arange(N_FIX))
    return result.reshape(N_FIX * BLK_DEV, TILES).astype(jnp.int32)


def level_of(stream_key, shape, cuts, smallest, high):
    factor_of, own = 1.0, jax.random.fold_in(stream_key, 6)
    for dim, shards_of in cuts:
        steps = jnp.exp(jax.random.uniform(jax.random.fold_in(own, dim), (shards_of,), jnp.float32, smallest / len(cuts), high / len(cuts)))
        factor_of = factor_of * jnp.repeat(steps, shape[dim] // shards_of).reshape([-1 if axis == dim else 1 for axis in range(len(shape))])
    return factor_of


def bell_draw(stream_key, shape, scale, most, cuts=(), kind=jnp.bfloat16):
    array = scale * jax.random.normal(stream_key, shape, jnp.float32)
    if cuts:
        array = array * level_of(stream_key, shape, cuts, -0.22, 0.18)
    return jnp.clip(array, -most, most).astype(kind)


def setup_inputs(seed: int = 0) -> dict:
    keys = jax.random.split(jax.random.key(seed), 8)
    fixels = bell_draw(keys[0], (FIXELS, SUBJ), 1.0, 6.0, ((0, 16), (1, 2)), jnp.float32)
    conn_tiles = bell_draw(keys[1], (FIX_BLOCKS, TILES, BS, BS), (BS * TILES) ** -0.5, 0.25, ((0, 16),), jnp.float32)
    columns = draw_columns(jax.random.fold_in(keys[7], 71), 0)
    nuisance = bell_draw(keys[3], (NUIS, SUBJ), 1.0, 5.0, ((1, 2),), jnp.float32)
    nuisance_pinv = bell_draw(keys[4], (NUIS, SUBJ), SUBJ ** -0.5, 0.375, ((1, 2),), jnp.float32)
    contrast = bell_draw(keys[5], (REGS, SUBJ), SUBJ ** -0.5, 0.375, (), jnp.float32)
    perm_table = jax.vmap(lambda own: jax.random.permutation(own, SUBJ))(jax.random.split(keys[6], PERMS)).reshape((PERMS, SUBJ)).astype(jnp.int32)
    return dict(fixels=fixels, conn_tiles=conn_tiles, columns=columns, nuisance=nuisance, nuisance_pinv=nuisance_pinv, contrast=contrast, perm_table=perm_table)


def reference(fixels, conn_tiles, columns, nuisance, nuisance_pinv, contrast, perm_table):
    blocks = fixels.reshape(-1, BS, SUBJ)

    def smooth(pieces):
        tile_row, column_row = pieces
        picked = jnp.take(blocks, column_row, axis=0)
        return jnp.einsum("kij,kjs->is", tile_row, picked, precision=lax.Precision.HIGHEST)

    smoothed = lax.map(smooth, (conn_tiles, columns)).reshape(-1, SUBJ)
    fitted = jnp.einsum("ns,fs->nf", nuisance_pinv, smoothed, precision=lax.Precision.HIGHEST)
    residual = smoothed - jnp.einsum("nf,ns->fs", fitted, nuisance, precision=lax.Precision.HIGHEST)
    design = jnp.transpose(jnp.take(contrast, perm_table, axis=1), (1, 0, 2)).reshape(PERMS * REGS, SUBJ)
    return jnp.einsum("cs,fs->cf", design, residual, precision=lax.Precision.HIGHEST)
```

```python
import functools

import jax
import jax.numpy as jnp
from jax import lax
from jax.experimental import pallas as pl
from jax.experimental.pallas import tpu as pltpu
from jax.sharding import PartitionSpec as P

GROUP = 4
LANES = 128
HIGHEST = lax.Precision.HIGHEST
ANY = pl.BlockSpec(memory_space=pl.ANY)
SMEM = pl.BlockSpec(memory_space=pltpu.SMEM)
VMEM = pl.BlockSpec(memory_space=pltpu.VMEM)


def pack_kernel(plan, piece_count, local_ref, line_ref, *refs):
    pieces = refs[:piece_count]
    outs = refs[piece_count:-1]
    sems = refs[-1]

    def copies(choice):
        return [
            pltpu.make_async_copy(
                pieces[choice if piece is None else piece].at[local_ref[entry]],
                outs[partner].at[place],
                sems.at[entry],
            )
            for entry, (piece, partner, place) in enumerate(plan)
        ]

    def run(choice):
        todo = copies(choice)
        for copy in todo:
            copy.start()
        for copy in todo:
            copy.wait()

    if plan[0][0] is None:
        upper = line_ref[0] != 0
        pl.when(upper)(lambda: run(0))
        pl.when(jnp.logical_not(upper))(lambda: run(1))
    else:
        run(0)


def pack(pieces, local, upper, cap, merged):
    groups, partners, _ = local.shape
    shape = pieces[0].shape[1:]
    plan = [
        (None if merged else piece, partner, piece * cap + rank)
        for piece in range(groups)
        for partner in range(partners)
        for rank in range(cap)
    ]
    size = groups * cap * partners * shape[0] * shape[1] * 4
    return pl.pallas_call(
        functools.partial(pack_kernel, plan, len(pieces)),
        out_shape=[jax.ShapeDtypeStruct((groups * cap,) + shape, jnp.float32)] * partners,
        in_specs=[SMEM, SMEM] + [ANY] * len(pieces),
        out_specs=[ANY] * partners,
        scratch_shapes=[pltpu.SemaphoreType.DMA((len(plan),))],
        cost_estimate=pl.CostEstimate(flops=0, bytes_accessed=2 * size, transcendentals=0),
    )(local.reshape(-1), upper, *pieces)


def split(value):
    high = value.astype(jnp.bfloat16)
    return high, (value - high.astype(jnp.float32)).astype(jnp.bfloat16)


def smooth_kernel(plan, per_row, source_count, first, tile_ref, local_ref, *refs):
    sources = refs[:source_count]
    conn = refs[source_count]
    before = None if first else refs[source_count + 1]
    out, blocks, tiles, here, sems = refs[source_count + (1 if first else 2) :]
    tile_total = blocks.shape[0]
    for t in range(tile_total):
        here[t] = 0
    for slot, (source, place) in enumerate(plan):
        tile = tile_ref[slot]

        @pl.when(tile >= 0)
        def _():
            index = local_ref[slot] if place is None else place
            here[tile] = 1
            pltpu.make_async_copy(
                sources[source].at[index], blocks.at[tile], sems.at[0, tile]
            ).start()
            pltpu.make_async_copy(conn.at[tile], tiles.at[tile], sems.at[1, tile]).start()

    if first:
        out[...] = jnp.zeros_like(out)
    else:
        out[...] = before[...]

    @pl.loop(0, tile_total)
    def _(t):
        @pl.when(here[t] != 0)
        def _():
            pltpu.make_async_copy(tiles.at[t], tiles.at[t], sems.at[1, t]).wait()
            pltpu.make_async_copy(blocks.at[t], blocks.at[t], sems.at[0, t]).wait()
            left_high, left_low = split(tiles[t])
            right_high, right_low = split(blocks[t])
            left = jnp.concatenate([left_high, left_low], axis=1)
            right = jnp.concatenate([right_high, right_low], axis=1)
            both = jnp.dot(
                left,
                jnp.concatenate([right, right], axis=0),
                preferred_element_type=jnp.float32,
            )
            width = blocks.shape[2]
            row = t // per_row
            out[row] += both[:, :width] + both[:, width:]


def smooth(plan, tile, local, sources, conn, before, block_count):
    tile_total, size, _ = conn.shape
    width = sources[0].shape[2]
    first = before is None
    extra = () if first else (before,)
    steps = min(tile_total, len(plan))
    return pl.pallas_call(
        functools.partial(
            smooth_kernel, plan, tile_total // block_count, len(sources), first
        ),
        out_shape=jax.ShapeDtypeStruct((block_count, size, width), jnp.float32),
        in_specs=[SMEM, SMEM] + [ANY] * (len(sources) + 1) + [VMEM] * len(extra),
        out_specs=VMEM,
        scratch_shapes=[
            pltpu.VMEM((tile_total, size, width), jnp.float32),
            pltpu.VMEM((tile_total, size, size), jnp.float32),
            pltpu.SMEM((tile_total,), jnp.int32),
            pltpu.SemaphoreType.DMA((2, tile_total)),
        ],
        compiler_params=pltpu.CompilerParams(vmem_limit_bytes=32 * 1024 * 1024),
        cost_estimate=pl.CostEstimate(
            flops=8 * steps * size * size * width,
            bytes_accessed=2 * steps * size * width * 4,
            transcendentals=0,
        ),
    )(tile, local, *sources, conn, *extra)


def design_kernel(perm_ref, contrast_ref, nuisance_ref, pinv_ref, out_ref, rows_ref):
    perms, subjects = perm_ref.shape
    regressors = contrast_ref.shape[0]
    for start in range(0, subjects, LANES):
        want = perm_ref[:, start : start + LANES].astype(jnp.int32)
        lane, part = want % LANES, want // LANES
        for r in range(regressors):
            value = jnp.zeros((perms, LANES), jnp.float32)
            for base in range(0, subjects, LANES):
                table = jnp.broadcast_to(
                    contrast_ref[r : r + 1, base : base + LANES], (perms, LANES)
                )
                found = jnp.take_along_axis(table, lane, axis=1, mode="promise_in_bounds")
                value = jnp.where(part == base // LANES, found, value)
            rows_ref[start // LANES, pl.ds(r, perms, stride=regressors), :] = value
    design = jnp.concatenate([rows_ref[i] for i in range(rows_ref.shape[0])], axis=1)
    result = design
    for n in range(nuisance_ref.shape[0]):
        weight = jnp.sum(design * nuisance_ref[n : n + 1, :], axis=1, keepdims=True)
        result = result - weight * pinv_ref[n : n + 1, :]
    out_ref[...] = result


def reduced_design(perm, contrast, nuisance, pinv):
    rows = perm.shape[0] * contrast.shape[0]
    subjects = perm.shape[1]
    return pl.pallas_call(
        design_kernel,
        out_shape=jax.ShapeDtypeStruct((rows, subjects), jnp.float32),
        in_specs=[VMEM] * 4,
        out_specs=VMEM,
        scratch_shapes=[pltpu.VMEM((subjects // LANES, rows, LANES), jnp.float32)],
        compiler_params=pltpu.CompilerParams(vmem_limit_bytes=32 * 1024 * 1024),
        cost_estimate=pl.CostEstimate(
            flops=32 * rows * subjects, bytes_accessed=8 * rows * subjects, transcendentals=0
        ),
    )(perm, contrast, nuisance, pinv)


def project(design, smoothed):
    return lax.dot_general(
        design, smoothed, (((1,), (1,)), ((), ())), precision=HIGHEST
    )


def per_device(fixels, conn_tiles, columns, nuisance, nuisance_pinv, contrast, perm_table):
    fix_count = lax.axis_size("fix")
    subj_count = lax.axis_size("subj")
    group = GROUP if fix_count % GROUP == 0 else 1
    lines = fix_count // group
    block_count, per_row = columns.shape
    size = conn_tiles.shape[2]
    width = fixels.shape[1]
    tile_total = block_count * per_row
    cap = (tile_total + fix_count - 1) // fix_count
    me = lax.axis_index("fix")
    line, member = me // group, me % group
    part = lax.axis_index("subj")

    own = fixels.reshape(block_count, size, width)
    up, down = {0: own}, {0: own}
    for hop in range(1, lines):
        up[hop] = lax.ppermute(
            up[hop - 1],
            "fix",
            [(i, i + group) for i in range(fix_count - group) if i // group >= hop - 1],
        )
        down[hop] = lax.ppermute(
            down[hop - 1],
            "fix",
            [(i, i - group) for i in range(group, fix_count) if i // group <= lines - hop],
        )

    named = [columns.reshape(-1)] + [
        lax.ppermute(columns, "fix", [(i, i ^ m) for i in range(fix_count)]).reshape(-1)
        for m in range(1, group)
    ]
    named = jnp.stack(named)
    owners, locals_ = named // block_count, named % block_count
    positions = jnp.arange(tile_total)
    earlier = positions[:, None] > positions[None, :]
    same = owners[:, :, None] == owners[:, None, :]
    ranks = jnp.sum(jnp.logical_and(same, earlier[None]).astype(jnp.int32), axis=2)
    rank_of = jnp.arange(cap)

    def lookup(who, owner_list, values):
        owner_list = jnp.asarray(owner_list)
        hit = jnp.logical_and(
            owners[who] == owner_list[..., None, None],
            ranks[who] == rank_of[:, None],
        )
        return jnp.sum(jnp.where(hit, values, 0), axis=-1)

    stages = []
    for hop in range(lines):
        if hop == 0:
            stages.append((hop, [own], [line], False))
        elif 2 * hop > lines - 1:
            far = jnp.where(line >= hop, line - hop, line + hop)
            stages.append((hop, [up[hop], down[hop]], [far], True))
        else:
            stages.append((hop, [up[hop], down[hop]], [line - hop, line + hop], False))

    early, late = ([], [], [], []), ([], [], [], [])
    for hop, pieces, origins, merged in stages:
        plan, tile, local, sources = late if hop == lines - 1 and hop > 0 else early
        upper = (line >= hop).astype(jnp.int32).reshape(1)
        asked = jnp.stack(
            [
                jnp.stack(
                    [lookup(m, origin * group + member, locals_[m]) for m in range(1, group)]
                )
                for origin in origins
            ]
        )
        packs = pack(pieces, asked, upper, cap, merged)
        sides = [z for z in range(lines) if z >= hop or z <= lines - 1 - hop]
        pairs = [(i, i) for i in range(fix_count) if i // group in sides]
        got = [
            lax.ppermute(packs[m - 1], "fix", [(i, i ^ m) for i, _ in pairs])
            for m in range(1, group)
        ]
        base = len(sources)
        sources.extend(pieces)
        sources.extend(got)
        own_tile = [lookup(0, origin * group + member, positions + 1) - 1 for origin in origins]
        own_local = [lookup(0, origin * group + member, locals_[0]) for origin in origins]
        for place, origin in enumerate(origins):
            for choice in range(2 if merged else 1):
                source = base + (choice if merged else place)
                for rank in range(cap):
                    plan.append((source, None))
                if merged:
                    mine = (line >= hop) if choice == 0 else (line < hop)
                    tile.append(jnp.where(mine, own_tile[place], -1))
                else:
                    tile.append(own_tile[place])
                local.append(own_local[place])
            for m in range(1, group):
                for rank in range(cap):
                    plan.append((base + len(pieces) + m - 1, place * cap + rank))
                tile.append(lookup(0, origin * group + (member ^ m), positions + 1) - 1)
                local.append(jnp.zeros((cap,), jnp.int32))

    conn = conn_tiles.reshape(tile_total, size, size)
    smoothed = None
    for plan, tile, local, sources in (early, late):
        if plan:
            smoothed = smooth(
                tuple(plan),
                jnp.concatenate(tile).astype(jnp.int32),
                jnp.concatenate(local).astype(jnp.int32),
                sources,
                conn,
                smoothed,
                block_count,
            )
    smoothed = smoothed.reshape(block_count * size, width)

    rows = perm_table.shape[0] // subj_count
    shares, halves = [], []
    for shift in range(subj_count):
        to = (part + shift) % subj_count
        share = jnp.concatenate(
            [
                lax.dynamic_slice_in_dim(perm_table, to * rows, rows, 0).astype(jnp.float32),
                nuisance,
                nuisance_pinv,
            ]
        )
        half = smoothed
        if shift:
            pairs = [(i, (i + shift) % subj_count) for i in range(subj_count)]
            share = lax.ppermute(share, "subj", pairs)
            half = lax.ppermute(half, "subj", pairs)
        shares.append(share)
        halves.append(half)
    shares = jnp.concatenate(shares, axis=1)
    count = nuisance.shape[0]
    design = reduced_design(
        shares[:rows],
        contrast,
        shares[rows : rows + count],
        shares[rows + count :],
    )
    total = None
    for shift, half in enumerate(halves):
        term = project(design[:, shift * width : (shift + 1) * width], half)
        total = term if total is None else total + term
    return total


def solution(mesh):
    placed = (
        P("fix", "subj"),
        P("fix", None, None, None),
        P("fix", None),
        P(None, "subj"),
        P(None, "subj"),
        P(),
        P(None, "subj"),
    )
    return jax.shard_map(
        per_device, mesh=mesh, in_specs=placed, out_specs=P("subj", "fix"), check_vma=False
    )
```

```python
import functools

import jax
import jax.numpy as jnp
from jax import lax
from jax.experimental import pallas as pl
from jax.experimental.pallas import tpu as pltpu
from jax.sharding import PartitionSpec as P

GROUP = 8
CHUNKS = 2
LANES = 128
ANY = pl.BlockSpec(memory_space=pl.ANY)
SMEM = pl.BlockSpec(memory_space=pltpu.SMEM)
VMEM = pl.BlockSpec(memory_space=pltpu.VMEM)
PARAMS = pltpu.CompilerParams(vmem_limit_bytes=32 * 1024 * 1024)


def cost(flops, bytes_accessed):
    return pl.CostEstimate(flops=flops, bytes_accessed=bytes_accessed, transcendentals=0)


def split(value):
    high = value.astype(jnp.bfloat16)
    return high, (value - high.astype(jnp.float32)).astype(jnp.bfloat16)


def turn_kernel(fixels_ref, *outs):
    block_count, sub, size = outs[0].shape
    for b in range(block_count):
        turned = fixels_ref[b * size : (b + 1) * size, :].T
        for c, out in enumerate(outs):
            out[b] = turned[c * sub : (c + 1) * sub, :]


def turn(fixels, block_count, sub):
    rows, width = fixels.shape
    shape = jax.ShapeDtypeStruct((block_count, sub, rows // block_count), jnp.float32)
    return pl.pallas_call(
        turn_kernel,
        out_shape=[shape] * (width // sub),
        in_specs=[VMEM],
        out_specs=[VMEM] * (width // sub),
        compiler_params=PARAMS,
        cost_estimate=cost(0, 8 * rows * width),
    )(fixels)


def tiles_kernel(conn_ref, out_ref):
    size = conn_ref.shape[1]

    @pl.loop(0, conn_ref.shape[0])
    def _(t):
        high, low = split(conn_ref[t])
        out_ref[t, :size, :] = high
        out_ref[t, size:, :] = low


def split_tiles(conn):
    total, size, _ = conn.shape
    return pl.pallas_call(
        tiles_kernel,
        out_shape=jax.ShapeDtypeStruct((total, 2 * size, size), jnp.bfloat16),
        in_specs=[VMEM],
        out_specs=VMEM,
        compiler_params=PARAMS,
        cost_estimate=cost(4 * total * size * size, 8 * total * size * size),
    )(conn)


def code_of(table_ref, place_ref, sizes, who, piece, other, rank):
    group, lines, cap = sizes
    line = lax.rem(lax.div(place_ref[0], group) + lines - piece, lines)
    member = jnp.bitwise_xor(lax.rem(place_ref[0], group), other)
    return table_ref[((who * lines + line) * group + member) * cap + rank]


def pack_kernel(piece_of, sizes, table_ref, place_ref, *refs):
    group, _, cap = sizes
    pieces = refs[: len(piece_of)]
    outs = refs[len(piece_of) : -1]
    sems = refs[-1]
    block_count = pieces[0].shape[0]
    todo = []
    for m in range(1, group):
        for item, piece in enumerate(piece_of):
            for rank in range(cap):
                code = code_of(table_ref, place_ref, sizes, m, piece, 0, rank)
                place = item * cap + rank
                copy = pltpu.make_async_copy(
                    pieces[item].at[lax.rem(jnp.maximum(code, 0), block_count)],
                    outs[m - 1].at[place],
                    sems.at[m - 1, place],
                )
                copy.start()
                todo.append(copy)
    for copy in todo:
        copy.wait()


def pack(items, table, place, sizes):
    group, _, cap = sizes
    piece_of, pieces = zip(*items)
    shape = pieces[0].shape[1:]
    count = cap * len(items)
    size = count * (group - 1) * shape[0] * shape[1] * 4
    return pl.pallas_call(
        functools.partial(pack_kernel, piece_of, sizes),
        out_shape=[jax.ShapeDtypeStruct((count,) + shape, jnp.float32)] * (group - 1),
        in_specs=[SMEM, SMEM] + [ANY] * len(items),
        out_specs=[VMEM] * (group - 1),
        scratch_shapes=[pltpu.SemaphoreType.DMA((group - 1, count))],
        compiler_params=PARAMS,
        cost_estimate=cost(0, 2 * size),
    )(table, place, *pieces)


def smooth_kernel(plan, sizes, per_row, source_count, table_ref, place_ref, *refs):
    sources = refs[:source_count]
    tiles_ref, out_ref, blocks, sems = refs[source_count:]
    tile_total, sub, size = blocks.shape
    block_count = tile_total // per_row
    for piece, m, source, base in plan:
        for rank in range(sizes[2]):
            code = code_of(table_ref, place_ref, sizes, 0, piece, m, rank)

            @pl.when(code >= 0)
            def _():
                tile, local = lax.div(code, block_count), lax.rem(code, block_count)
                pltpu.make_async_copy(
                    sources[source].at[local if m == 0 else base + rank],
                    blocks.at[tile],
                    sems.at[tile],
                ).start()

    for row in range(block_count):
        highs, lows = [], []
        for tile in range(row * per_row, (row + 1) * per_row):
            pltpu.make_async_copy(blocks.at[tile], blocks.at[tile], sems.at[tile]).wait()
            high, low = split(blocks[tile])
            highs.append(high)
            lows.append(low)
        left = jnp.concatenate(
            [jnp.concatenate(highs, axis=1), jnp.concatenate(lows, axis=1)], axis=0
        )
        right = jnp.concatenate(
            [tiles_ref[tile] for tile in range(row * per_row, (row + 1) * per_row)], axis=1
        )
        terms = lax.dot_general(
            left, right, (((1,), (1,)), ((), ())), preferred_element_type=jnp.float32
        )
        value = (terms[:sub, :size] + terms[sub:, :size]) + (
            terms[:sub, size:] + terms[sub:, size:]
        )
        out_ref[:, row * size : (row + 1) * size] = value


def smooth(plan, sizes, table, place, sources, tiles, block_count):
    tile_total, _, size = tiles.shape
    sub = sources[0].shape[1]
    return pl.pallas_call(
        functools.partial(
            smooth_kernel, plan, sizes, tile_total // block_count, len(sources)
        ),
        out_shape=jax.ShapeDtypeStruct((sub, block_count * size), jnp.float32),
        in_specs=[SMEM, SMEM] + [ANY] * len(sources) + [VMEM],
        out_specs=VMEM,
        scratch_shapes=[
            pltpu.VMEM((tile_total, sub, size), jnp.float32),
            pltpu.SemaphoreType.DMA((tile_total,)),
        ],
        compiler_params=PARAMS,
        cost_estimate=cost(
            8 * tile_total * size * size * sub, 4 * tile_total * size * (sub + size)
        ),
    )(table, place, *sources, tiles)


def design_kernel(sub, perm_ref, contrast_ref, nuisance_ref, pinv_ref, out_ref, rows_ref):
    perms, subjects = perm_ref.shape
    regressors = contrast_ref.shape[0]
    for start in range(0, subjects, LANES):
        want = perm_ref[:, start : start + LANES].astype(jnp.int32)
        lane, part = want % LANES, want // LANES
        for r in range(regressors):
            value = jnp.zeros((perms, LANES), jnp.float32)
            for base in range(0, subjects, LANES):
                table = jnp.broadcast_to(
                    contrast_ref[r : r + 1, base : base + LANES], (perms, LANES)
                )
                found = jnp.take_along_axis(table, lane, axis=1, mode="promise_in_bounds")
                value = jnp.where(part == base // LANES, found, value)
            rows_ref[start // LANES, pl.ds(r, perms, stride=regressors), :] = value
    design = jnp.concatenate([rows_ref[i] for i in range(rows_ref.shape[0])], axis=1)
    result = design
    for n in range(nuisance_ref.shape[0]):
        weight = jnp.sum(design * nuisance_ref[n : n + 1, :], axis=1, keepdims=True)
        result = result - weight * pinv_ref[n : n + 1, :]
    high, low = split(result)
    for q in range(subjects // sub):
        columns = slice(q * sub, (q + 1) * sub)
        out_ref[q] = jnp.concatenate(
            [high[:, columns], high[:, columns], low[:, columns], low[:, columns]], axis=1
        )


def reduced_design(perm, contrast, nuisance, pinv, sub):
    rows = perm.shape[0] * contrast.shape[0]
    subjects = perm.shape[1]
    return pl.pallas_call(
        functools.partial(design_kernel, sub),
        out_shape=jax.ShapeDtypeStruct((subjects // sub, rows, 4 * sub), jnp.bfloat16),
        in_specs=[VMEM] * 4,
        out_specs=VMEM,
        scratch_shapes=[pltpu.VMEM((subjects // LANES, rows, LANES), jnp.float32)],
        compiler_params=PARAMS,
        cost_estimate=cost(32 * rows * subjects, 8 * rows * subjects),
    )(perm, contrast, nuisance, pinv)


def project_kernel(chunks, first, design_ref, *refs):
    parts = refs[: len(chunks)]
    before = None if first else refs[len(chunks)]
    out_ref = refs[-1]
    total = None if first else before[...]
    for q, part in zip(chunks, parts):
        high, low = split(part[...])
        term = jnp.dot(
            design_ref[q],
            jnp.concatenate([high, low, high, low], axis=0),
            preferred_element_type=jnp.float32,
        )
        total = term if total is None else total + term
    out_ref[...] = total


def project(design, chunks, parts, before):
    _, rows, _ = design.shape
    sub, fixels = parts[0].shape
    step = 256
    first = before is None
    wide = pl.BlockSpec((sub, step), lambda i: (0, i))
    tall = pl.BlockSpec((rows, step), lambda i: (0, i))
    return pl.pallas_call(
        functools.partial(project_kernel, tuple(chunks), first),
        grid=(fixels // step,),
        out_shape=jax.ShapeDtypeStruct((rows, fixels), jnp.float32),
        in_specs=[pl.BlockSpec(design.shape, lambda i: (0, 0, 0))]
        + [wide] * len(parts)
        + ([] if first else [tall]),
        out_specs=tall,
        compiler_params=PARAMS,
        cost_estimate=cost(
            8 * len(parts) * rows * sub * fixels, 4 * fixels * (rows + sub * len(parts))
        ),
    )(design, *parts, *(() if first else (before,)))


def per_device(fixels, conn_tiles, columns, nuisance, nuisance_pinv, contrast, perm_table):
    fix_count = lax.axis_size("fix")
    subj_count = lax.axis_size("subj")
    group = GROUP if fix_count % GROUP == 0 else 1
    lines = fix_count // group
    block_count, per_row = columns.shape
    size = conn_tiles.shape[2]
    width = fixels.shape[1]
    sub = width // CHUNKS
    tile_total = block_count * per_row
    cap = (tile_total + fix_count - 1) // fix_count
    sizes = (group, lines, cap)
    me = lax.axis_index("fix")
    part = lax.axis_index("subj")
    place = me.astype(jnp.int32).reshape(1)

    own = turn(fixels, block_count, sub)
    pieces = [
        [own[c]]
        + [
            lax.ppermute(
                own[c],
                "fix",
                [(i, (i + k * group) % fix_count) for i in range(fix_count)],
            )
            for k in range(1, lines)
        ]
        for c in range(CHUNKS)
    ]

    named = columns.reshape(1, tile_total)
    step = 1
    while step < group:
        pairs = [(i, i ^ step) for i in range(fix_count)]
        named = jnp.concatenate([named, lax.ppermute(named, "fix", pairs)])
        step *= 2
    owners = named // block_count
    positions = jnp.arange(tile_total)
    earlier = positions[:, None] > positions[None, :]
    same = owners[:, :, None] == owners[:, None, :]
    ranks = jnp.sum(jnp.logical_and(same, earlier[None]).astype(jnp.int32), axis=2)
    slots = (owners * cap + ranks)[:, None, :] == jnp.arange(fix_count * cap)[:, None]
    codes = (positions * block_count + named % block_count + 1)[:, None, :]
    table = (jnp.sum(jnp.where(slots, codes, 0), axis=2) - 1).astype(jnp.int32).reshape(-1)

    rows = perm_table.shape[0] // subj_count
    count = nuisance.shape[0]
    shares = []
    for shift in range(subj_count):
        to = (part + shift) % subj_count
        share = jnp.concatenate(
            [
                lax.dynamic_slice_in_dim(perm_table, to * rows, rows, 0).astype(jnp.float32),
                nuisance,
                nuisance_pinv,
            ]
        )
        if shift:
            pairs = [(i, (i + shift) % subj_count) for i in range(subj_count)]
            share = lax.ppermute(share, "subj", pairs)
        shares.append(share)
    shares = jnp.concatenate(shares, axis=1)
    design = reduced_design(
        shares[:rows], contrast, shares[rows : rows + count], shares[rows + count :], sub
    )

    tiles = split_tiles(conn_tiles.reshape(tile_total, size, size))
    smoothed = []
    for c in range(CHUNKS):
        packs = pack(list(enumerate(pieces[c])), table, place, sizes)
        got = [
            lax.ppermute(packs[m - 1], "fix", [(i, i ^ m) for i in range(fix_count)])
            for m in range(1, group)
        ]
        plan = []
        for k in range(lines):
            plan.append((k, 0, k, 0))
            plan.extend((k, m, lines + m - 1, k * cap) for m in range(1, group))
        smoothed.append(
            smooth(tuple(plan), sizes, table, place, pieces[c] + got, tiles, block_count)
        )

    total = project(design, range(CHUNKS), smoothed, None)
    for shift in range(1, subj_count):
        pairs = [(i, (i + shift) % subj_count) for i in range(subj_count)]
        halves = [lax.ppermute(value, "subj", pairs) for value in smoothed]
        chunks = range(shift * CHUNKS, (shift + 1) * CHUNKS)
        total = project(design, chunks, halves, total)
    return total


def solution(mesh):
    placed = (
        P("fix", "subj"),
        P("fix", None, None, None),
        P("fix", None),
        P(None, "subj"),
        P(None, "subj"),
        P(),
        P(None, "subj"),
    )
    return jax.shard_map(
        per_device, mesh=mesh, in_specs=placed, out_specs=P("subj", "fix"), check_vma=False
    )
```

```python
import functools

import jax
import jax.numpy as jnp
from jax import lax
from jax.experimental import pallas as pl
from jax.experimental.pallas import tpu as pltpu
from jax.sharding import PartitionSpec as P

GROUP = 8
SHARES = (1, 1)
GATE = 2
LANES = 128
ANY = pl.BlockSpec(memory_space=pl.ANY)
SMEM = pl.BlockSpec(memory_space=pltpu.SMEM)
VMEM = pl.BlockSpec(memory_space=pltpu.VMEM)
PARAMS = pltpu.CompilerParams(vmem_limit_bytes=16 * 1024 * 1024)


def cost(flops, bytes_accessed):
    return pl.CostEstimate(flops=flops, bytes_accessed=bytes_accessed, transcendentals=0)


def split(value):
    high = value.astype(jnp.bfloat16)
    return high, (value - high.astype(jnp.float32)).astype(jnp.bfloat16)


def turn_kernel(fixels_ref, out_ref):
    block_count, _, size = out_ref.shape
    for b in range(block_count):
        out_ref[b] = fixels_ref[b * size : (b + 1) * size, :].T


def turn(fixels, block_count):
    rows, width = fixels.shape
    return pl.pallas_call(
        turn_kernel,
        out_shape=jax.ShapeDtypeStruct((block_count, width, rows // block_count), jnp.float32),
        in_specs=[VMEM],
        out_specs=VMEM,
        compiler_params=PARAMS,
        cost_estimate=cost(0, 8 * rows * width),
    )(fixels)


def copy_kernel(value_ref, *refs):
    refs[-1][...] = value_ref[...]


def follow(value, after):
    return pl.pallas_call(
        copy_kernel,
        out_shape=jax.ShapeDtypeStruct(value.shape, value.dtype),
        in_specs=[VMEM] + [ANY] * len(after),
        out_specs=VMEM,
        compiler_params=PARAMS,
        cost_estimate=cost(0, 8 * value.size),
    )(value, *after)


def tiles_kernel(conn_ref, out_ref):
    size = conn_ref.shape[1]
    for t in range(conn_ref.shape[0]):
        high, low = split(conn_ref[t].T)
        out_ref[t, :, :size] = high
        out_ref[t, :, size:] = low


def split_tiles(conn):
    total, size, _ = conn.shape
    return pl.pallas_call(
        tiles_kernel,
        out_shape=jax.ShapeDtypeStruct((total, size, 2 * size), jnp.bfloat16),
        in_specs=[VMEM],
        out_specs=VMEM,
        compiler_params=PARAMS,
        cost_estimate=cost(4 * total * size * size, 8 * total * size * size),
    )(conn)


def pack_kernel(entries, cuts, table_ref, *refs):
    pieces = refs[: len(entries[0])]
    outs = refs[len(pieces) :]
    for partner, columns in enumerate(entries):
        at = 0
        for piece, places in zip(pieces, columns):
            for place in places:
                block = piece[table_ref[1, place]]
                for cut, (start, sub) in enumerate(cuts):
                    outs[partner * len(cuts) + cut][at] = block[start : start + sub, :]
                at += 1


def pack(entries, cuts, pieces, table):
    count = len(entries[0][0]) * len(pieces)
    size = pieces[0].shape[2]
    outs = [
        jax.ShapeDtypeStruct((count, sub, size), jnp.float32) for _ in entries for _, sub in cuts
    ]
    return pl.pallas_call(
        functools.partial(pack_kernel, entries, cuts),
        out_shape=outs,
        in_specs=[SMEM] + [VMEM] * len(pieces),
        out_specs=[VMEM] * len(outs),
        compiler_params=PARAMS,
        cost_estimate=cost(0, 8 * sum(out.size for out in outs)),
    )(table, *pieces)


def smooth_kernel(plan, per_row, source_count, table_ref, *refs):
    sources = refs[:source_count]
    tiles_ref, out_ref, highs, lows = refs[source_count:]
    sub, size = highs.shape[1:]
    block_count = out_ref.shape[1] // size
    for place, source, at, start in plan:
        block = sources[source][table_ref[1, place] if at is None else at]
        tile = table_ref[0, place]
        highs[tile], lows[tile] = split(block[start : start + sub, :])

    for row in range(block_count):
        span = range(row * per_row, (row + 1) * per_row)
        left = jnp.concatenate(
            [
                jnp.concatenate([highs[tile] for tile in span], axis=1),
                jnp.concatenate([lows[tile] for tile in span], axis=1),
            ],
            axis=0,
        )
        right = jnp.concatenate([tiles_ref[tile] for tile in span], axis=0)
        terms = jnp.dot(left, right, preferred_element_type=jnp.float32)
        value = (terms[:sub, :size] + terms[sub:, :size]) + (
            terms[:sub, size:] + terms[sub:, size:]
        )
        out_ref[:, row * size : (row + 1) * size] = value


def smooth(plan, table, sources, sub, tiles, block_count):
    tile_total, size, _ = tiles.shape
    return pl.pallas_call(
        functools.partial(smooth_kernel, plan, tile_total // block_count, len(sources)),
        out_shape=jax.ShapeDtypeStruct((sub, block_count * size), jnp.float32),
        in_specs=[SMEM] + [VMEM] * (len(sources) + 1),
        out_specs=VMEM,
        scratch_shapes=[pltpu.VMEM((tile_total + 1, sub, size), jnp.bfloat16)] * 2,
        compiler_params=PARAMS,
        cost_estimate=cost(
            8 * tile_total * size * size * sub, 4 * tile_total * size * (sub + size)
        ),
    )(table, *sources, tiles)


def design_kernel(cuts, perm_ref, contrast_ref, nuisance_ref, pinv_ref, *refs):
    outs, rows_ref = refs[:-1], refs[-1]
    perms, subjects = perm_ref.shape
    regressors = contrast_ref.shape[0]
    for start in range(0, subjects, LANES):
        want = perm_ref[:, start : start + LANES].astype(jnp.int32)
        lane, part = want % LANES, want // LANES
        for r in range(regressors):
            value = jnp.zeros((perms, LANES), jnp.float32)
            for base in range(0, subjects, LANES):
                table = jnp.broadcast_to(
                    contrast_ref[r : r + 1, base : base + LANES], (perms, LANES)
                )
                found = jnp.take_along_axis(table, lane, axis=1, mode="promise_in_bounds")
                value = jnp.where(part == base // LANES, found, value)
            rows_ref[start // LANES, pl.ds(r, perms, stride=regressors), :] = value
    design = jnp.concatenate([rows_ref[i] for i in range(rows_ref.shape[0])], axis=1)
    result = design
    for n in range(nuisance_ref.shape[0]):
        weight = jnp.sum(design * nuisance_ref[n : n + 1, :], axis=1, keepdims=True)
        result = result - weight * pinv_ref[n : n + 1, :]
    high, low = split(result)
    for (start, sub), out in zip(cuts, outs):
        columns = slice(start, start + sub)
        out[...] = jnp.concatenate(
            [high[:, columns], high[:, columns], low[:, columns], low[:, columns]], axis=1
        )


def reduced_design(perm, contrast, nuisance, pinv, cuts):
    rows = perm.shape[0] * contrast.shape[0]
    subjects = perm.shape[1]
    return pl.pallas_call(
        functools.partial(design_kernel, cuts),
        out_shape=[jax.ShapeDtypeStruct((rows, 4 * sub), jnp.bfloat16) for _, sub in cuts],
        in_specs=[VMEM] * 4,
        out_specs=[VMEM] * len(cuts),
        scratch_shapes=[pltpu.VMEM((subjects // LANES, rows, LANES), jnp.float32)],
        compiler_params=PARAMS,
        cost_estimate=cost(32 * rows * subjects, 8 * rows * subjects),
    )(perm, contrast, nuisance, pinv)


def project_kernel(count, step, last, *refs):
    designs, parts = refs[:count], refs[count : 2 * count]
    before = refs[2 * count : -3] if last else refs[2 * count : -1]
    out_ref = refs[-3] if last else refs[-1]
    fixels = out_ref.shape[1]
    copies = []
    for i, start in enumerate(range(0, fixels, step)):
        span = slice(start, start + step)
        total = before[0][:, span] if before else None
        for design, part in zip(designs, parts):
            high, low = split(part[:, span])
            term = jnp.dot(
                design[...],
                jnp.concatenate([high, low, high, low], axis=0),
                preferred_element_type=jnp.float32,
            )
            total = term if total is None else total + term
        if last:
            held, sems = refs[-2:]
            held[i] = total
            copy = pltpu.make_async_copy(held.at[i], out_ref.at[:, span], sems.at[i])
            copy.start()
            copies.append(copy)
        else:
            out_ref[:, span] = total
    for copy in copies:
        copy.wait()


def project(designs, parts, before, last):
    rows = designs[0].shape[0]
    fixels = parts[0].shape[1]
    step = 256
    steps = fixels // step
    scratch = [pltpu.VMEM((steps, rows, step), jnp.float32), pltpu.SemaphoreType.DMA((steps,))]
    return pl.pallas_call(
        functools.partial(project_kernel, len(parts), step, last),
        out_shape=jax.ShapeDtypeStruct((rows, fixels), jnp.float32),
        in_specs=[VMEM] * (2 * len(parts) + len(before)),
        out_specs=ANY if last else VMEM,
        scratch_shapes=scratch if last else [],
        compiler_params=PARAMS,
        cost_estimate=cost(
            8 * rows * fixels * sum(part.shape[0] for part in parts), 8 * fixels * rows
        ),
    )(*designs, *parts, *before)


def per_device(fixels, conn_tiles, columns, nuisance, nuisance_pinv, contrast, perm_table):
    fix_count = lax.axis_size("fix")
    subj_count = lax.axis_size("subj")
    group = GROUP if fix_count % GROUP == 0 else 1
    lines = fix_count // group
    block_count, per_row = columns.shape
    size = conn_tiles.shape[2]
    width = fixels.shape[1]
    subs = [width * share // sum(SHARES) for share in SHARES]
    starts = [sum(subs[:c]) for c in range(len(subs))]
    tile_total = block_count * per_row
    cap = (tile_total + fix_count - 1) // fix_count
    me = lax.axis_index("fix")
    part = lax.axis_index("subj")

    def swap(value, mask):
        return lax.ppermute(value, "fix", [(i, i ^ mask) for i in range(fix_count)])

    own = turn(fixels, block_count)
    beside = swap(own, 1)
    sent = follow(columns.T, [beside])
    partners = range(group - 2, 0, -2)
    named = jnp.stack([sent.reshape(-1)] + [swap(sent, m).reshape(-1) for m in partners])
    positions = jnp.arange(tile_total)
    earlier = positions[:, None] > positions[None, :]
    owners = named // block_count
    same = owners[:, :, None] == owners[:, None, :]
    ranks = jnp.sum(jnp.logical_and(same, earlier[None]).astype(jnp.int32), axis=2)
    order = jnp.arange(fix_count * cap)
    owner = (me // group + lines - order // (group * cap)) % lines * group + (
        (me % group) ^ (order // cap % group)
    )
    hits = (owners * cap + ranks)[:, None, :] == (owner * cap + order % cap)[:, None]
    tile = positions % block_count * per_row + positions // block_count
    codes = (tile - tile_total) * block_count + named % block_count
    codes = jnp.sum(jnp.where(hits, codes[:, None, :], 0), axis=2).reshape(-1)
    codes = codes + tile_total * block_count
    table = jnp.stack([codes // block_count, codes % block_count]).astype(jnp.int32)

    def places(row, k, other):
        base = ((row * lines + k) * group + other) * cap
        return tuple(range(base, base + cap))

    rows = perm_table.shape[0] // subj_count
    count = nuisance.shape[0]
    shares = []
    for shift in range(subj_count):
        to = (part + shift) % subj_count
        share = jnp.concatenate(
            [
                lax.dynamic_slice_in_dim(perm_table, to * rows, rows, 0).astype(jnp.float32),
                nuisance,
                nuisance_pinv,
            ]
        )
        if shift:
            pairs = [(i, (i + shift) % subj_count) for i in range(subj_count)]
            share = lax.ppermute(share, "subj", pairs)
        shares.append(share)
    shares = jnp.concatenate(shares, axis=1)
    cuts = [
        (shift * width + start, sub)
        for shift in range(subj_count)
        for start, sub in zip(starts, subs)
    ]
    design = reduced_design(
        shares[:rows], contrast, shares[rows : rows + count], shares[rows + count :], cuts
    )

    tiles = split_tiles(conn_tiles.reshape(tile_total, size, size))

    def exchange(pieces, k, cuts, base):
        entries = tuple(
            tuple(places(row, k, e) for e in range(2)) for row in range(1, len(partners) + 1)
        )
        packs = pack(entries, cuts, pieces, table)
        got = [
            [swap(packs[i * len(cuts) + c], m) for i, m in enumerate(partners)]
            for c in range(len(cuts))
        ]
        plan = []
        for e in range(2):
            plan.extend((place, base + e, None) for place in places(0, k, e))
            for source, m in enumerate(partners, base + 2):
                plan.extend(
                    (place, source, e * cap + rank)
                    for rank, place in enumerate(places(0, k, m ^ e))
                )
        return got, plan

    pieces = [own, beside]
    (got,), plan = exchange(pieces, 0, ((0, width),), 0)
    gate = got[GATE:] + [design[0], tiles]
    whole = pieces + got
    plans = [[(place, source, at, start) for place, source, at in plan] for start in starts]
    sources = [list(whole) for _ in subs]
    for k in range(1, lines):
        pairs = [(i, (i + k * group) % fix_count) for i in range(fix_count)]
        piece = follow(lax.ppermute(own, "fix", pairs), gate)
        pieces = [piece, swap(piece, 1)]
        got, plan = exchange(pieces, k, tuple(zip(starts, subs)), len(sources[0]))
        for c, start in enumerate(starts):
            plans[c].extend(
                (place, source, at, start if at is None else 0) for place, source, at in plan
            )
            sources[c].extend(pieces + got[c])
    smoothed = [
        smooth(tuple(plans[c]), table, sources[c], sub, tiles, block_count)
        for c, sub in enumerate(subs)
    ]

    parts = list(smoothed)
    for shift in range(1, subj_count):
        pairs = [(i, (i + shift) % subj_count) for i in range(subj_count)]
        parts.extend(lax.ppermute(value, "subj", pairs) for value in smoothed)
    total = project(design[:-1], parts[:-1], [], False)
    return project(design[-1:], parts[-1:], [total], True)


def solution(mesh):
    placed = (
        P("fix", "subj"),
        P("fix", None, None, None),
        P("fix", None),
        P(None, "subj"),
        P(None, "subj"),
        P(),
        P(None, "subj"),
    )
    return jax.shard_map(
        per_device, mesh=mesh, in_specs=placed, out_specs=P("subj", "fix"), check_vma=False
    )
```

```python
import functools

import jax
import jax.numpy as jnp
import numpy as np
from jax import lax
from jax.experimental import pallas as pl
from jax.experimental.pallas import tpu as pltpu
from jax.sharding import PartitionSpec as P

GROUP = 8
SHARES = (5, 3)
LANES = 128
ANY = pl.BlockSpec(memory_space=pl.ANY)
SMEM = pl.BlockSpec(memory_space=pltpu.SMEM)
VMEM = pl.BlockSpec(memory_space=pltpu.VMEM)
PARAMS = pltpu.CompilerParams(vmem_limit_bytes=16 * 1024 * 1024)


def cost(flops, bytes_accessed):
    return pl.CostEstimate(flops=flops, bytes_accessed=bytes_accessed, transcendentals=0)


def split(value):
    high = value.astype(jnp.bfloat16)
    return high, (value - high.astype(jnp.float32)).astype(jnp.bfloat16)


def follow_kernel(*refs):
    pass


def follow(value, after):
    return pl.pallas_call(
        follow_kernel,
        out_shape=jax.ShapeDtypeStruct(value.shape, value.dtype),
        in_specs=[ANY] * (1 + len(after)),
        out_specs=ANY,
        input_output_aliases={0: 0},
        compiler_params=PARAMS,
        cost_estimate=cost(0, 0),
    )(value, *after)


def copy_kernel(value_ref, *refs):
    refs[-1][...] = value_ref[...]


def follow_copy(value, after):
    return pl.pallas_call(
        copy_kernel,
        out_shape=jax.ShapeDtypeStruct(value.shape, value.dtype),
        in_specs=[VMEM] + [ANY] * len(after),
        out_specs=VMEM,
        compiler_params=PARAMS,
        cost_estimate=cost(0, 8 * value.size),
    )(value, *after)


def tiles_kernel(conn_ref, out_ref):
    size = conn_ref.shape[1]
    for t in range(conn_ref.shape[0]):
        high, low = split(conn_ref[t].T)
        out_ref[t, :, :size] = high
        out_ref[t, :, size:] = low


def split_tiles(conn):
    total, size, _ = conn.shape
    return pl.pallas_call(
        tiles_kernel,
        out_shape=jax.ShapeDtypeStruct((total, size, 2 * size), jnp.bfloat16),
        in_specs=[VMEM],
        out_specs=VMEM,
        compiler_params=PARAMS,
        cost_estimate=cost(4 * total * size * size, 8 * total * size * size),
    )(conn)


def pack_kernel(lists, cap, counts, base_ref, *refs):
    table_count, piece_count = counts
    tables, pieces = refs[:table_count], refs[table_count : table_count + piece_count]
    outs = refs[-len(lists) :]
    for entries, out in zip(lists, outs):
        at = 0
        for piece, table, row, owner, start, sub in entries:
            for rank in range(cap):
                block = pieces[piece][tables[table][row, base_ref[owner] + rank]]
                out[at : at + sub, :] = block.T[start : start + sub, :]
                at += sub


def pack(lists, cap, bases, tables, pieces, after):
    size = pieces[0].shape[1]
    outs = [
        jax.ShapeDtypeStruct(
            (sum(cap * sub for _, _, _, _, _, sub in entries), size), jnp.float32
        )
        for entries in lists
    ]
    return pl.pallas_call(
        functools.partial(pack_kernel, lists, cap, (len(tables), len(pieces))),
        out_shape=outs,
        in_specs=[SMEM] * (1 + len(tables)) + [VMEM] * len(pieces) + [ANY] * len(after),
        out_specs=[VMEM] * len(outs),
        compiler_params=PARAMS,
        cost_estimate=cost(0, 8 * sum(out.size for out in outs)),
    )(bases, *tables, *pieces, *after)


def smooth_kernel(plan, per_row, source_count, table_ref, *refs):
    sources = refs[:source_count]
    tiles_ref, out_ref, highs, lows = refs[source_count:]
    sub, size = highs.shape[1:]
    block_count = out_ref.shape[1] // size
    for place, source, at in plan:
        tile = table_ref[place]
        highs[tile], lows[tile] = split(sources[source][at : at + sub, :])

    for row in range(block_count):
        span = range(row * per_row, (row + 1) * per_row)
        left = jnp.concatenate(
            [
                jnp.concatenate([highs[tile] for tile in span], axis=1),
                jnp.concatenate([lows[tile] for tile in span], axis=1),
            ],
            axis=0,
        )
        right = jnp.concatenate([tiles_ref[tile] for tile in span], axis=0)
        terms = jnp.dot(left, right, preferred_element_type=jnp.float32)
        value = (terms[:sub, :size] + terms[sub:, :size]) + (
            terms[:sub, size:] + terms[sub:, size:]
        )
        out_ref[:, row * size : (row + 1) * size] = value


def smooth(plan, table, sources, sub, tiles, block_count):
    tile_total, size, _ = tiles.shape
    return pl.pallas_call(
        functools.partial(smooth_kernel, plan, tile_total // block_count, len(sources)),
        out_shape=jax.ShapeDtypeStruct((sub, block_count * size), jnp.float32),
        in_specs=[SMEM] + [VMEM] * (len(sources) + 1),
        out_specs=VMEM,
        scratch_shapes=[pltpu.VMEM((tile_total + 1, sub, size), jnp.bfloat16)] * 2,
        compiler_params=PARAMS,
        cost_estimate=cost(
            8 * tile_total * size * size * sub, 4 * tile_total * size * (sub + size)
        ),
    )(table, *sources, tiles)


def design_kernel(cuts, perm_ref, contrast_ref, nuisance_ref, pinv_ref, *refs):
    outs, rows_ref = refs[:-1], refs[-1]
    perms, subjects = perm_ref.shape
    regressors = contrast_ref.shape[0]
    for start in range(0, subjects, LANES):
        want = perm_ref[:, start : start + LANES].astype(jnp.int32)
        lane, part = want % LANES, want // LANES
        for r in range(regressors):
            value = jnp.zeros((perms, LANES), jnp.float32)
            for base in range(0, subjects, LANES):
                table = jnp.broadcast_to(
                    contrast_ref[r : r + 1, base : base + LANES], (perms, LANES)
                )
                found = jnp.take_along_axis(table, lane, axis=1, mode="promise_in_bounds")
                value = jnp.where(part == base // LANES, found, value)
            rows_ref[start // LANES, pl.ds(r, perms, stride=regressors), :] = value
    design = jnp.concatenate([rows_ref[i] for i in range(rows_ref.shape[0])], axis=1)
    result = design
    for n in range(nuisance_ref.shape[0]):
        weight = jnp.sum(design * nuisance_ref[n : n + 1, :], axis=1, keepdims=True)
        result = result - weight * pinv_ref[n : n + 1, :]
    high, low = split(result)
    for (start, sub), out in zip(cuts, outs):
        columns = slice(start, start + sub)
        out[...] = jnp.concatenate(
            [high[:, columns], high[:, columns], low[:, columns], low[:, columns]], axis=1
        )


def reduced_design(perm, contrast, nuisance, pinv, cuts):
    rows = perm.shape[0] * contrast.shape[0]
    subjects = perm.shape[1]
    return pl.pallas_call(
        functools.partial(design_kernel, cuts),
        out_shape=[jax.ShapeDtypeStruct((rows, 4 * sub), jnp.bfloat16) for _, sub in cuts],
        in_specs=[VMEM] * 4,
        out_specs=[VMEM] * len(cuts),
        scratch_shapes=[pltpu.VMEM((subjects // LANES, rows, LANES), jnp.float32)],
        compiler_params=PARAMS,
        cost_estimate=cost(32 * rows * subjects, 8 * rows * subjects),
    )(perm, contrast, nuisance, pinv)


def project_kernel(count, step, last, *refs):
    designs, parts = refs[:count], refs[count : 2 * count]
    before = refs[2 * count : -3] if last else refs[2 * count : -1]
    out_ref = refs[-3] if last else refs[-1]
    fixels = out_ref.shape[1]
    copies = []
    for i, start in enumerate(range(0, fixels, step)):
        span = slice(start, start + step)
        total = before[0][:, span] if before else None
        for design, part in zip(designs, parts):
            high, low = split(part[:, span])
            term = jnp.dot(
                design[...],
                jnp.concatenate([high, low, high, low], axis=0),
                preferred_element_type=jnp.float32,
            )
            total = term if total is None else total + term
        if last:
            held, sems = refs[-2:]
            held[i] = total
            copy = pltpu.make_async_copy(held.at[i], out_ref.at[:, span], sems.at[i])
            copy.start()
            copies.append(copy)
        else:
            out_ref[:, span] = total
    for copy in copies:
        copy.wait()


def project(designs, parts, before, last):
    rows = designs[0].shape[0]
    fixels = parts[0].shape[1]
    step = 256
    steps = fixels // step
    scratch = [pltpu.VMEM((steps, rows, step), jnp.float32), pltpu.SemaphoreType.DMA((steps,))]
    return pl.pallas_call(
        functools.partial(project_kernel, len(parts), step, last),
        out_shape=jax.ShapeDtypeStruct((rows, fixels), jnp.float32),
        in_specs=[VMEM] * (2 * len(parts) + len(before)),
        out_specs=ANY if last else VMEM,
        scratch_shapes=scratch if last else [],
        compiler_params=PARAMS,
        cost_estimate=cost(
            8 * rows * fixels * sum(part.shape[0] for part in parts), 8 * fixels * rows
        ),
    )(*designs, *parts, *before)


def per_device(fixels, conn_tiles, columns, nuisance, nuisance_pinv, contrast, perm_table):
    fix_count = lax.axis_size("fix")
    subj_count = lax.axis_size("subj")
    group = GROUP if fix_count % GROUP == 0 else 1
    lines = fix_count // group
    block_count, per_row = columns.shape
    size = conn_tiles.shape[2]
    width = fixels.shape[1]
    subs = [width * share // sum(SHARES) for share in SHARES]
    starts = [sum(subs[:c]) for c in range(len(subs))]
    tile_total = block_count * per_row
    cap = (tile_total + fix_count - 1) // fix_count
    me = lax.axis_index("fix")
    part = lax.axis_index("subj")

    def swap(value, mask):
        return lax.ppermute(value, "fix", [(i, i ^ mask) for i in range(fix_count)])

    named = columns.T.reshape(-1)
    positions = jnp.arange(tile_total)
    owners, blocks = named // block_count, named % block_count
    earlier = jnp.logical_and(
        owners[:, None] == owners[None, :], positions[:, None] > positions[None, :]
    )
    slots = owners * cap + jnp.sum(earlier.astype(jnp.int32), axis=1)
    order = jnp.arange(fix_count * cap)
    hits = slots == order[:, None]
    request = jnp.sum(jnp.where(hits, blocks, 0), axis=1).reshape(1, -1).astype(jnp.int32)
    line, member = me // group, me % group
    near_first = (line + lines - np.arange(lines)) % lines * group
    bases = ((near_first[:, None] + (member ^ np.arange(group))) * cap).reshape(-1)
    bases = bases.astype(jnp.int32)
    owner = jnp.repeat(bases, cap) + order % cap
    tile = positions % block_count * per_row + positions // block_count
    table = jnp.sum(jnp.where(slots == owner[:, None], tile - tile_total, 0), axis=1)
    table = (table + tile_total).astype(jnp.int32)

    def places(k, other):
        base = (k * group + other) * cap
        return tuple(range(base, base + cap))

    raw = fixels.reshape(block_count, size, width)
    far_raw = {}
    for k in range(1, lines):
        pairs = [(i, (i + k * group) % fix_count) for i in range(fix_count)]
        far_raw[k] = lax.ppermute(raw, "fix", pairs)
    across_raw = {m: swap(raw, m) for m in range(4, group, 4)}
    beside = swap(raw, 1)
    asked = {2: (swap(request, 2), 0)}
    both_requests = jnp.concatenate([request, asked[2][0]])
    for m in range(4, group, 4):
        pair = swap(both_requests, m)
        asked[m], asked[m + 2] = (pair, 0), (pair, 1)

    perm_table = follow_copy(perm_table, [asked[2][0]])
    rows = perm_table.shape[0] // subj_count
    count = nuisance.shape[0]
    shares = []
    for shift in range(subj_count):
        to = (part + shift) % subj_count
        share = jnp.concatenate(
            [
                lax.dynamic_slice_in_dim(perm_table, to * rows, rows, 0).astype(jnp.float32),
                nuisance,
                nuisance_pinv,
            ]
        )
        if shift:
            pairs = [(i, (i + shift) % subj_count) for i in range(subj_count)]
            share = lax.ppermute(share, "subj", pairs)
        shares.append(share)
    shares = jnp.concatenate(shares, axis=1)
    cuts = [
        (shift * width + start, sub)
        for shift in range(subj_count)
        for start, sub in zip(starts, subs)
    ]
    design = reduced_design(
        shares[:rows], contrast, shares[rows : rows + count], shares[rows + count :], cuts
    )

    tiles = split_tiles(conn_tiles.reshape(tile_total, size, size))

    plans, sources = [[] for _ in subs], [[] for _ in subs]

    def pick(chosen, after):
        pieces, tables, lists = [], [], []
        for index, (m, items, start, count) in enumerate(chosen):
            row = asked[m][1] if m else 0
            lists.append(
                tuple(
                    (len(pieces) + i, index, row, key[0] * group + key[1], start, count)
                    for i, key in enumerate(items)
                )
            )
            pieces.extend(items.values())
            tables.append(asked[m][0] if m else request)
        packs = pack(tuple(lists), cap, bases, tables, pieces, after)
        got = [swap(value, m) if m else value for value, (m, *_) in zip(packs, chosen)]
        for value, (m, items, start, count) in zip(got, chosen):
            for c, sub in enumerate(subs):
                if start <= starts[c] and starts[c] + sub <= start + count:
                    for i, (k, other) in enumerate(items):
                        for rank, place in enumerate(places(k, other ^ m)):
                            at = (i * cap + rank) * count + starts[c] - start
                            plans[c].append((place, len(sources[c]), at))
                    sources[c].append(value)
        return got

    near = {(0, 0): raw, (0, 1): beside}
    after = pick([(2, near, 0, width)], [])
    after = after + [design[0], tiles] + [asked[m][0] for m in range(4, group, 4)]
    arrived = {(k, 0): value for k, value in far_raw.items()}
    arrived.update({(0, m): value for m, value in across_raw.items()})
    arrived = {key: follow(value, after) for key, value in arrived.items()}
    second = {(k, m ^ 1): swap(value, 1) for (k, m), value in arrived.items()}
    everything = {**arrived, **second}
    far = {key: value for key, value in everything.items() if key[0]}
    others = [(m, far) for m in range(4, group, 2)]
    sooner = pick([(2, arrived, 0, subs[0])], [])
    later = pick([(m, items, 0, subs[0]) for m, items in [(2, second)] + others], [])
    after = (sooner[:1] + later[:0])
    for start, sub in list(zip(starts, subs))[1:]:
        pick([(m, items, start, sub) for m, items in [(2, everything)] + others], after)
    pick([(0, {**near, **arrived, **second}, 0, width)], [])
    smoothed = [
        smooth(tuple(plans[c]), table, sources[c], sub, tiles, block_count)
        for c, sub in enumerate(subs)
    ]
    parts = list(smoothed)
    for shift in range(1, subj_count):
        pairs = [(i, (i + shift) % subj_count) for i in range(subj_count)]
        parts.extend(lax.ppermute(value, "subj", pairs) for value in smoothed)
    total = project(design[:-1], parts[:-1], [], False)
    return project(design[-1:], parts[-1:], [total], True)


def solution(mesh):
    placed = (
        P("fix", "subj"),
        P("fix", None, None, None),
        P("fix", None),
        P(None, "subj"),
        P(None, "subj"),
        P(),
        P(None, "subj"),
    )
    return jax.shard_map(
        per_device, mesh=mesh, in_specs=placed, out_specs=P("subj", "fix"), check_vma=False
    )
```

```python
import functools

import jax
import jax.numpy as jnp
import numpy as np
from jax import lax
from jax.experimental import pallas as pl
from jax.experimental.pallas import tpu as pltpu
from jax.sharding import PartitionSpec as P

GROUP = 8
SHARES = (5, 3)
LANES = 128
ANY = pl.BlockSpec(memory_space=pl.ANY)
SMEM = pl.BlockSpec(memory_space=pltpu.SMEM)
VMEM = pl.BlockSpec(memory_space=pltpu.VMEM)
PARAMS = pltpu.CompilerParams(vmem_limit_bytes=16 * 1024 * 1024)


def cost(flops, bytes_accessed):
    return pl.CostEstimate(flops=flops, bytes_accessed=bytes_accessed, transcendentals=0)


def split(value):
    high = value.astype(jnp.bfloat16)
    return high, (value - high.astype(jnp.float32)).astype(jnp.bfloat16)


def follow_kernel(*refs):
    pass


def follow(value, after):
    return pl.pallas_call(
        follow_kernel,
        out_shape=jax.ShapeDtypeStruct(value.shape, value.dtype),
        in_specs=[ANY] * (1 + len(after)),
        out_specs=ANY,
        input_output_aliases={0: 0},
        compiler_params=PARAMS,
        cost_estimate=cost(0, 0),
    )(value, *after)


def copy_kernel(value_ref, *refs):
    refs[-1][...] = value_ref[...]


def follow_copy(value, after):
    return pl.pallas_call(
        copy_kernel,
        out_shape=jax.ShapeDtypeStruct(value.shape, value.dtype),
        in_specs=[VMEM] + [ANY] * len(after),
        out_specs=VMEM,
        compiler_params=PARAMS,
        cost_estimate=cost(0, 8 * value.size),
    )(value, *after)


def tiles_kernel(conn_ref, out_ref):
    size = conn_ref.shape[1]
    for t in range(conn_ref.shape[0]):
        high, low = split(conn_ref[t].T)
        out_ref[t, :, :size] = high
        out_ref[t, :, size:] = low


def split_tiles(conn):
    total, size, _ = conn.shape
    return pl.pallas_call(
        tiles_kernel,
        out_shape=jax.ShapeDtypeStruct((total, size, 2 * size), jnp.bfloat16),
        in_specs=[VMEM],
        out_specs=VMEM,
        compiler_params=PARAMS,
        cost_estimate=cost(4 * total * size * size, 8 * total * size * size),
    )(conn)


def pack_kernel(lists, cap, counts, base_ref, *refs):
    table_count, piece_count = counts
    tables, pieces = refs[:table_count], refs[table_count : table_count + piece_count]
    outs = refs[-len(lists) :]
    for entries, out in zip(lists, outs):
        at = 0
        for piece, table, row, owner, start, sub in entries:
            for rank in range(cap):
                block = pieces[piece][tables[table][row, base_ref[owner] + rank]]
                out[at : at + sub, :] = block.T[start : start + sub, :]
                at += sub


def pack(lists, cap, bases, tables, pieces, after):
    size = pieces[0].shape[1]
    outs = [
        jax.ShapeDtypeStruct(
            (sum(cap * sub for _, _, _, _, _, sub in entries), size), jnp.float32
        )
        for entries in lists
    ]
    return pl.pallas_call(
        functools.partial(pack_kernel, lists, cap, (len(tables), len(pieces))),
        out_shape=outs,
        in_specs=[SMEM] * (1 + len(tables)) + [VMEM] * len(pieces) + [ANY] * len(after),
        out_specs=[VMEM] * len(outs),
        compiler_params=PARAMS,
        cost_estimate=cost(0, 8 * sum(out.size for out in outs)),
    )(bases, *tables, *pieces, *after)


def smooth_kernel(plan, per_row, source_count, table_ref, *refs):
    sources = refs[:source_count]
    tiles_ref, out_ref, highs, lows = refs[source_count:]
    sub, size = highs.shape[1:]
    block_count = out_ref.shape[1] // size
    for place, source, at in plan:
        tile = table_ref[place]
        highs[tile], lows[tile] = split(sources[source][at : at + sub, :])

    for row in range(block_count):
        span = range(row * per_row, (row + 1) * per_row)
        left = jnp.concatenate(
            [
                jnp.concatenate([highs[tile] for tile in span], axis=1),
                jnp.concatenate([lows[tile] for tile in span], axis=1),
            ],
            axis=0,
        )
        right = jnp.concatenate([tiles_ref[tile] for tile in span], axis=0)
        terms = jnp.dot(left, right, preferred_element_type=jnp.float32)
        value = (terms[:sub, :size] + terms[sub:, :size]) + (
            terms[:sub, size:] + terms[sub:, size:]
        )
        out_ref[:, row * size : (row + 1) * size] = value


def smooth(plan, table, sources, sub, tiles, block_count):
    tile_total, size, _ = tiles.shape
    return pl.pallas_call(
        functools.partial(smooth_kernel, plan, tile_total // block_count, len(sources)),
        out_shape=jax.ShapeDtypeStruct((sub, block_count * size), jnp.float32),
        in_specs=[SMEM] + [VMEM] * (len(sources) + 1),
        out_specs=VMEM,
        scratch_shapes=[pltpu.VMEM((tile_total + 1, sub, size), jnp.bfloat16)] * 2,
        compiler_params=PARAMS,
        cost_estimate=cost(
            8 * tile_total * size * size * sub, 4 * tile_total * size * (sub + size)
        ),
    )(table, *sources, tiles)


def design_kernel(cuts, perm_ref, contrast_ref, nuisance_ref, pinv_ref, *refs):
    outs, rows_ref = refs[:-1], refs[-1]
    perms, subjects = perm_ref.shape
    regressors = contrast_ref.shape[0]
    for start in range(0, subjects, LANES):
        want = perm_ref[:, start : start + LANES].astype(jnp.int32)
        lane, part = want % LANES, want // LANES
        for r in range(regressors):
            value = jnp.zeros((perms, LANES), jnp.float32)
            for base in range(0, subjects, LANES):
                table = jnp.broadcast_to(
                    contrast_ref[r : r + 1, base : base + LANES], (perms, LANES)
                )
                found = jnp.take_along_axis(table, lane, axis=1, mode="promise_in_bounds")
                value = jnp.where(part == base // LANES, found, value)
            rows_ref[start // LANES, pl.ds(r, perms, stride=regressors), :] = value
    design = jnp.concatenate([rows_ref[i] for i in range(rows_ref.shape[0])], axis=1)
    result = design
    for n in range(nuisance_ref.shape[0]):
        weight = jnp.sum(design * nuisance_ref[n : n + 1, :], axis=1, keepdims=True)
        result = result - weight * pinv_ref[n : n + 1, :]
    high, low = split(result)
    for (start, sub), out in zip(cuts, outs):
        columns = slice(start, start + sub)
        out[...] = jnp.concatenate(
            [high[:, columns], high[:, columns], low[:, columns], low[:, columns]], axis=1
        )


def reduced_design(perm, contrast, nuisance, pinv, cuts):
    rows = perm.shape[0] * contrast.shape[0]
    subjects = perm.shape[1]
    return pl.pallas_call(
        functools.partial(design_kernel, cuts),
        out_shape=[jax.ShapeDtypeStruct((rows, 4 * sub), jnp.bfloat16) for _, sub in cuts],
        in_specs=[VMEM] * 4,
        out_specs=[VMEM] * len(cuts),
        scratch_shapes=[pltpu.VMEM((subjects // LANES, rows, LANES), jnp.float32)],
        compiler_params=PARAMS,
        cost_estimate=cost(32 * rows * subjects, 8 * rows * subjects),
    )(perm, contrast, nuisance, pinv)


def project_kernel(count, step, last, *refs):
    designs, parts = refs[:count], refs[count : 2 * count]
    before = refs[2 * count : -3] if last else refs[2 * count : -1]
    out_ref = refs[-3] if last else refs[-1]
    fixels = out_ref.shape[1]
    copies = []
    for i, start in enumerate(range(0, fixels, step)):
        span = slice(start, start + step)
        total = before[0][:, span] if before else None
        for design, part in zip(designs, parts):
            high, low = split(part[:, span])
            term = jnp.dot(
                design[...],
                jnp.concatenate([high, low, high, low], axis=0),
                preferred_element_type=jnp.float32,
            )
            total = term if total is None else total + term
        if last:
            held, sems = refs[-2:]
            held[i] = total
            copy = pltpu.make_async_copy(held.at[i], out_ref.at[:, span], sems.at[i])
            copy.start()
            copies.append(copy)
        else:
            out_ref[:, span] = total
    for copy in copies:
        copy.wait()


def project(designs, parts, before, last):
    rows = designs[0].shape[0]
    fixels = parts[0].shape[1]
    step = 256
    steps = fixels // step
    scratch = [pltpu.VMEM((steps, rows, step), jnp.float32), pltpu.SemaphoreType.DMA((steps,))]
    return pl.pallas_call(
        functools.partial(project_kernel, len(parts), step, last),
        out_shape=jax.ShapeDtypeStruct((rows, fixels), jnp.float32),
        in_specs=[VMEM] * (2 * len(parts) + len(before)),
        out_specs=ANY if last else VMEM,
        scratch_shapes=scratch if last else [],
        compiler_params=PARAMS,
        cost_estimate=cost(
            8 * rows * fixels * sum(part.shape[0] for part in parts), 8 * fixels * rows
        ),
    )(*designs, *parts, *before)


def per_device(fixels, conn_tiles, columns, nuisance, nuisance_pinv, contrast, perm_table):
    fix_count = lax.axis_size("fix")
    subj_count = lax.axis_size("subj")
    group = GROUP if fix_count % GROUP == 0 else 1
    lines = fix_count // group
    block_count, per_row = columns.shape
    size = conn_tiles.shape[2]
    width = fixels.shape[1]
    subs = [width * share // sum(SHARES) for share in SHARES]
    starts = [sum(subs[:c]) for c in range(len(subs))]
    tile_total = block_count * per_row
    cap = (tile_total + fix_count - 1) // fix_count
    me = lax.axis_index("fix")
    part = lax.axis_index("subj")

    def swap(value, mask):
        return lax.ppermute(value, "fix", [(i, i ^ mask) for i in range(fix_count)])

    named = columns.T.reshape(-1)
    positions = jnp.arange(tile_total)
    owners, blocks = named // block_count, named % block_count
    earlier = jnp.logical_and(
        owners[:, None] == owners[None, :], positions[:, None] > positions[None, :]
    )
    slots = owners * cap + jnp.sum(earlier.astype(jnp.int32), axis=1)
    order = jnp.arange(fix_count * cap)
    hits = slots == order[:, None]
    request = jnp.sum(jnp.where(hits, blocks, 0), axis=1).reshape(1, -1).astype(jnp.int32)
    line, member = me // group, me % group
    near_first = (line + lines - np.arange(lines)) % lines * group
    bases = ((near_first[:, None] + (member ^ np.arange(group))) * cap).reshape(-1)
    bases = bases.astype(jnp.int32)
    owner = jnp.repeat(bases, cap) + order % cap
    tile = positions % block_count * per_row + positions // block_count
    table = jnp.sum(jnp.where(slots == owner[:, None], tile - tile_total, 0), axis=1)
    table = (table + tile_total).astype(jnp.int32)

    def places(k, other):
        base = (k * group + other) * cap
        return tuple(range(base, base + cap))

    raw = fixels.reshape(block_count, size, width)
    across_raw = {m: swap(raw, m) for m in range(4, group, 4)}
    far_raw = {}
    for k in range(1, lines):
        pairs = [(i, (i + k * group) % fix_count) for i in range(fix_count)]
        far_raw[k] = lax.ppermute(raw, "fix", pairs)
    beside = swap(raw, 1)
    asked = {2: (swap(request, 2), 0)}
    both_requests = jnp.concatenate([request, asked[2][0]])
    for m in range(4, group, 4):
        pair = swap(both_requests, m)
        asked[m], asked[m + 2] = (pair, 0), (pair, 1)

    perm_table = follow_copy(perm_table, [asked[2][0]])
    rows = perm_table.shape[0] // subj_count
    count = nuisance.shape[0]
    shares = []
    for shift in range(subj_count):
        to = (part + shift) % subj_count
        share = jnp.concatenate(
            [
                lax.dynamic_slice_in_dim(perm_table, to * rows, rows, 0).astype(jnp.float32),
                nuisance,
                nuisance_pinv,
            ]
        )
        if shift:
            pairs = [(i, (i + shift) % subj_count) for i in range(subj_count)]
            share = lax.ppermute(share, "subj", pairs)
        shares.append(share)
    shares = jnp.concatenate(shares, axis=1)
    cuts = [
        (shift * width + start, sub)
        for shift in range(subj_count)
        for start, sub in zip(starts, subs)
    ]
    design = reduced_design(
        shares[:rows], contrast, shares[rows : rows + count], shares[rows + count :], cuts
    )

    tiles = split_tiles(conn_tiles.reshape(tile_total, size, size))

    plans, sources = [[] for _ in subs], [[] for _ in subs]

    def pick(chosen, after):
        pieces, tables, lists = [], [], []
        for index, (m, items, start, count) in enumerate(chosen):
            row = asked[m][1] if m else 0
            lists.append(
                tuple(
                    (len(pieces) + i, index, row, key[0] * group + key[1], start, count)
                    for i, key in enumerate(items)
                )
            )
            pieces.extend(items.values())
            tables.append(asked[m][0] if m else request)
        packs = pack(tuple(lists), cap, bases, tables, pieces, after)
        got = [swap(value, m) if m else value for value, (m, *_) in zip(packs, chosen)]
        for value, (m, items, start, count) in zip(got, chosen):
            for c, sub in enumerate(subs):
                if start <= starts[c] and starts[c] + sub <= start + count:
                    for i, (k, other) in enumerate(items):
                        for rank, place in enumerate(places(k, other ^ m)):
                            at = (i * cap + rank) * count + starts[c] - start
                            plans[c].append((place, len(sources[c]), at))
                    sources[c].append(value)
        return got

    near = {(0, 0): raw, (0, 1): beside}
    after = pick([(2, near, 0, width)], [])
    after = after + [design[0], tiles] + [asked[m][0] for m in range(4, group, 4)]
    arrived = {(0, m): value for m, value in across_raw.items()}
    arrived.update({(k, 0): value for k, value in far_raw.items()})
    arrived = {key: follow(value, after) for key, value in arrived.items()}
    second = {(k, m ^ 1): swap(value, 1) for (k, m), value in arrived.items()}
    everything = {**arrived, **second}
    far = {key: value for key, value in everything.items() if key[0]}
    others = [(m, far) for m in range(4, group, 2)]
    pick([(m, far, 0, subs[0]) for m in (6, 4)], [])
    sooner = pick([(2, arrived, 0, subs[0])], [])
    pick([(2, second, 0, subs[0])], [])
    for start, sub in list(zip(starts, subs))[1:]:
        pick([(m, items, start, sub) for m, items in [(2, everything)] + others], [])
    pick([(0, {**near, **arrived, **second}, 0, width)], [])
    smoothed = [
        smooth(tuple(plans[c]), table, sources[c], sub, tiles, block_count)
        for c, sub in enumerate(subs)
    ]
    parts = list(smoothed)
    for shift in range(1, subj_count):
        pairs = [(i, (i + shift) % subj_count) for i in range(subj_count)]
        parts.extend(lax.ppermute(value, "subj", pairs) for value in smoothed)
    total = project(design[:-1], parts[:-1], [], False)
    return project(design[-1:], parts[-1:], [total], True)


def solution(mesh):
    placed = (
        P("fix", "subj"),
        P("fix", None, None, None),
        P("fix", None),
        P(None, "subj"),
        P(None, "subj"),
        P(),
        P(None, "subj"),
    )
    return jax.shard_map(
        per_device, mesh=mesh, in_specs=placed, out_specs=P("subj", "fix"), check_vma=False
    )
```

```python
import functools

import jax
import jax.numpy as jnp
import numpy as np
from jax import lax
from jax.experimental import pallas as pl
from jax.experimental.pallas import tpu as pltpu
from jax.sharding import PartitionSpec as P

GROUP = 8
SHARES = (1, 1)
LANES = 128
ANY = pl.BlockSpec(memory_space=pl.ANY)
SMEM = pl.BlockSpec(memory_space=pltpu.SMEM)
VMEM = pl.BlockSpec(memory_space=pltpu.VMEM)
PARAMS = pltpu.CompilerParams(vmem_limit_bytes=16 * 1024 * 1024)


def cost(flops, bytes_accessed):
    return pl.CostEstimate(flops=flops, bytes_accessed=bytes_accessed, transcendentals=0)


def split(value):
    high = value.astype(jnp.bfloat16)
    return high, (value - high.astype(jnp.float32)).astype(jnp.bfloat16)


def follow_kernel(*refs):
    pass


def follow(value, after):
    return pl.pallas_call(
        follow_kernel,
        out_shape=jax.ShapeDtypeStruct(value.shape, value.dtype),
        in_specs=[ANY] * (1 + len(after)),
        out_specs=ANY,
        input_output_aliases={0: 0},
        compiler_params=PARAMS,
        cost_estimate=cost(0, 0),
    )(value, *after)


def copy_kernel(value_ref, *refs):
    refs[-1][...] = value_ref[...]


def follow_copy(value, after):
    return pl.pallas_call(
        copy_kernel,
        out_shape=jax.ShapeDtypeStruct(value.shape, value.dtype),
        in_specs=[VMEM] + [ANY] * len(after),
        out_specs=VMEM,
        compiler_params=PARAMS,
        cost_estimate=cost(0, 8 * value.size),
    )(value, *after)


def tiles_kernel(conn_ref, out_ref):
    size = conn_ref.shape[1]
    for t in range(conn_ref.shape[0]):
        high, low = split(conn_ref[t].T)
        out_ref[t, :, :size] = high
        out_ref[t, :, size:] = low


def split_tiles(conn):
    total, size, _ = conn.shape
    return pl.pallas_call(
        tiles_kernel,
        out_shape=jax.ShapeDtypeStruct((total, size, 2 * size), jnp.bfloat16),
        in_specs=[VMEM],
        out_specs=VMEM,
        compiler_params=PARAMS,
        cost_estimate=cost(4 * total * size * size, 8 * total * size * size),
    )(conn)


def pack_kernel(lists, cap, counts, base_ref, *refs):
    table_count, piece_count = counts
    tables, pieces = refs[:table_count], refs[table_count : table_count + piece_count]
    outs = refs[-len(lists) :]
    for entries, out in zip(lists, outs):
        at = 0
        for piece, table, row, owner, start, sub in entries:
            for rank in range(cap):
                block = pieces[piece][tables[table][row, base_ref[owner] + rank]]
                out[at : at + sub, :] = block.T[start : start + sub, :]
                at += sub


def pack(lists, cap, bases, tables, pieces, after):
    size = pieces[0].shape[1]
    outs = [
        jax.ShapeDtypeStruct(
            (sum(cap * sub for _, _, _, _, _, sub in entries), size), jnp.float32
        )
        for entries in lists
    ]
    return pl.pallas_call(
        functools.partial(pack_kernel, lists, cap, (len(tables), len(pieces))),
        out_shape=outs,
        in_specs=[SMEM] * (1 + len(tables)) + [VMEM] * len(pieces) + [ANY] * len(after),
        out_specs=[VMEM] * len(outs),
        compiler_params=PARAMS,
        cost_estimate=cost(0, 8 * sum(out.size for out in outs)),
    )(bases, *tables, *pieces, *after)


def smooth_kernel(plan, per_row, source_count, table_ref, *refs):
    sources = refs[:source_count]
    tiles_ref, out_ref, highs, lows = refs[source_count:]
    sub, size = highs.shape[1:]
    block_count = out_ref.shape[1] // size
    for place, source, at in plan:
        tile = table_ref[place]
        highs[tile], lows[tile] = split(sources[source][at : at + sub, :])

    for row in range(block_count):
        span = range(row * per_row, (row + 1) * per_row)
        left = jnp.concatenate(
            [
                jnp.concatenate([highs[tile] for tile in span], axis=1),
                jnp.concatenate([lows[tile] for tile in span], axis=1),
            ],
            axis=0,
        )
        right = jnp.concatenate([tiles_ref[tile] for tile in span], axis=0)
        terms = jnp.dot(left, right, preferred_element_type=jnp.float32)
        value = (terms[:sub, :size] + terms[sub:, :size]) + (
            terms[:sub, size:] + terms[sub:, size:]
        )
        out_ref[:, row * size : (row + 1) * size] = value


def smooth(plan, table, sources, sub, tiles, block_count):
    tile_total, size, _ = tiles.shape
    return pl.pallas_call(
        functools.partial(smooth_kernel, plan, tile_total // block_count, len(sources)),
        out_shape=jax.ShapeDtypeStruct((sub, block_count * size), jnp.float32),
        in_specs=[SMEM] + [VMEM] * (len(sources) + 1),
        out_specs=VMEM,
        scratch_shapes=[pltpu.VMEM((tile_total + 1, sub, size), jnp.bfloat16)] * 2,
        compiler_params=PARAMS,
        cost_estimate=cost(
            8 * tile_total * size * size * sub, 4 * tile_total * size * (sub + size)
        ),
    )(table, *sources, tiles)


def design_kernel(cuts, perm_ref, contrast_ref, nuisance_ref, pinv_ref, *refs):
    outs, rows_ref = refs[:-1], refs[-1]
    perms, subjects = perm_ref.shape
    regressors = contrast_ref.shape[0]
    for start in range(0, subjects, LANES):
        want = perm_ref[:, start : start + LANES].astype(jnp.int32)
        lane, part = want % LANES, want // LANES
        for r in range(regressors):
            value = jnp.zeros((perms, LANES), jnp.float32)
            for base in range(0, subjects, LANES):
                table = jnp.broadcast_to(
                    contrast_ref[r : r + 1, base : base + LANES], (perms, LANES)
                )
                found = jnp.take_along_axis(table, lane, axis=1, mode="promise_in_bounds")
                value = jnp.where(part == base // LANES, found, value)
            rows_ref[start // LANES, pl.ds(r, perms, stride=regressors), :] = value
    design = jnp.concatenate([rows_ref[i] for i in range(rows_ref.shape[0])], axis=1)
    result = design
    for n in range(nuisance_ref.shape[0]):
        weight = jnp.sum(design * nuisance_ref[n : n + 1, :], axis=1, keepdims=True)
        result = result - weight * pinv_ref[n : n + 1, :]
    high, low = split(result)
    for (start, sub), out in zip(cuts, outs):
        columns = slice(start, start + sub)
        out[...] = jnp.concatenate(
            [high[:, columns], high[:, columns], low[:, columns], low[:, columns]], axis=1
        )


def reduced_design(perm, contrast, nuisance, pinv, cuts):
    rows = perm.shape[0] * contrast.shape[0]
    subjects = perm.shape[1]
    return pl.pallas_call(
        functools.partial(design_kernel, cuts),
        out_shape=[jax.ShapeDtypeStruct((rows, 4 * sub), jnp.bfloat16) for _, sub in cuts],
        in_specs=[VMEM] * 4,
        out_specs=[VMEM] * len(cuts),
        scratch_shapes=[pltpu.VMEM((subjects // LANES, rows, LANES), jnp.float32)],
        compiler_params=PARAMS,
        cost_estimate=cost(32 * rows * subjects, 8 * rows * subjects),
    )(perm, contrast, nuisance, pinv)


def project_kernel(count, step, last, *refs):
    designs, parts = refs[:count], refs[count : 2 * count]
    before = refs[2 * count : -3] if last else refs[2 * count : -1]
    out_ref = refs[-3] if last else refs[-1]
    fixels = out_ref.shape[1]
    copies = []
    for i, start in enumerate(range(0, fixels, step)):
        span = slice(start, start + step)
        total = before[0][:, span] if before else None
        for design, part in zip(designs, parts):
            high, low = split(part[:, span])
            term = jnp.dot(
                design[...],
                jnp.concatenate([high, low, high, low], axis=0),
                preferred_element_type=jnp.float32,
            )
            total = term if total is None else total + term
        if last:
            held, sems = refs[-2:]
            held[i] = total
            copy = pltpu.make_async_copy(held.at[i], out_ref.at[:, span], sems.at[i])
            copy.start()
            copies.append(copy)
        else:
            out_ref[:, span] = total
    for copy in copies:
        copy.wait()


def project(designs, parts, before, last):
    rows = designs[0].shape[0]
    fixels = parts[0].shape[1]
    step = 256
    steps = fixels // step
    scratch = [pltpu.VMEM((steps, rows, step), jnp.float32), pltpu.SemaphoreType.DMA((steps,))]
    return pl.pallas_call(
        functools.partial(project_kernel, len(parts), step, last),
        out_shape=jax.ShapeDtypeStruct((rows, fixels), jnp.float32),
        in_specs=[VMEM] * (2 * len(parts) + len(before)),
        out_specs=ANY if last else VMEM,
        scratch_shapes=scratch if last else [],
        compiler_params=PARAMS,
        cost_estimate=cost(
            8 * rows * fixels * sum(part.shape[0] for part in parts), 8 * fixels * rows
        ),
    )(*designs, *parts, *before)


def per_device(fixels, conn_tiles, columns, nuisance, nuisance_pinv, contrast, perm_table):
    fix_count = lax.axis_size("fix")
    subj_count = lax.axis_size("subj")
    group = GROUP if fix_count % GROUP == 0 else 1
    lines = fix_count // group
    block_count, per_row = columns.shape
    size = conn_tiles.shape[2]
    width = fixels.shape[1]
    subs = [width * share // sum(SHARES) for share in SHARES]
    starts = [sum(subs[:c]) for c in range(len(subs))]
    tile_total = block_count * per_row
    cap = (tile_total + fix_count - 1) // fix_count
    me = lax.axis_index("fix")
    part = lax.axis_index("subj")

    def swap(value, mask):
        return lax.ppermute(value, "fix", [(i, i ^ mask) for i in range(fix_count)])

    named = columns.T.reshape(-1)
    positions = jnp.arange(tile_total)
    owners, blocks = named // block_count, named % block_count
    earlier = jnp.logical_and(
        owners[:, None] == owners[None, :], positions[:, None] > positions[None, :]
    )
    slots = owners * cap + jnp.sum(earlier.astype(jnp.int32), axis=1)
    order = jnp.arange(fix_count * cap)
    hits = slots == order[:, None]
    request = jnp.sum(jnp.where(hits, blocks, 0), axis=1).reshape(1, -1).astype(jnp.int32)
    line, member = me // group, me % group
    near_first = (line + lines - np.arange(lines)) % lines * group
    bases = ((near_first[:, None] + (member ^ np.arange(group))) * cap).reshape(-1)
    bases = bases.astype(jnp.int32)
    owner = jnp.repeat(bases, cap) + order % cap
    tile = positions % block_count * per_row + positions // block_count
    table = jnp.sum(jnp.where(slots == owner[:, None], tile - tile_total, 0), axis=1)
    table = (table + tile_total).astype(jnp.int32)

    def places(k, other):
        base = (k * group + other) * cap
        return tuple(range(base, base + cap))

    raw = fixels.reshape(block_count, size, width)
    across_raw = {m: swap(raw, m) for m in range(4, group, 4)}
    far_raw = {}
    for k in range(1, lines):
        pairs = [(i, (i + k * group) % fix_count) for i in range(fix_count)]
        far_raw[k] = lax.ppermute(raw, "fix", pairs)
    beside = swap(raw, 1)
    asked = {2: (swap(request, 2), 0)}
    both_requests = jnp.concatenate([request, asked[2][0]])
    for m in range(4, group, 4):
        pair = swap(both_requests, m)
        asked[m], asked[m + 2] = (pair, 0), (pair, 1)

    perm_table = follow_copy(perm_table, [asked[2][0]])
    rows = perm_table.shape[0] // subj_count
    count = nuisance.shape[0]
    shares = []
    for shift in range(subj_count):
        to = (part + shift) % subj_count
        share = jnp.concatenate(
            [
                lax.dynamic_slice_in_dim(perm_table, to * rows, rows, 0).astype(jnp.float32),
                nuisance,
                nuisance_pinv,
            ]
        )
        if shift:
            pairs = [(i, (i + shift) % subj_count) for i in range(subj_count)]
            share = lax.ppermute(share, "subj", pairs)
        shares.append(share)
    shares = jnp.concatenate(shares, axis=1)
    cuts = [
        (shift * width + start, sub)
        for shift in range(subj_count)
        for start, sub in zip(starts, subs)
    ]
    design = reduced_design(
        shares[:rows], contrast, shares[rows : rows + count], shares[rows + count :], cuts
    )

    tiles = split_tiles(conn_tiles.reshape(tile_total, size, size))

    plans, sources = [[] for _ in subs], [[] for _ in subs]

    def pick(chosen, after):
        pieces, tables, lists = [], [], []
        for index, (m, items, start, count) in enumerate(chosen):
            row = asked[m][1] if m else 0
            lists.append(
                tuple(
                    (len(pieces) + i, index, row, key[0] * group + key[1], start, count)
                    for i, key in enumerate(items)
                )
            )
            pieces.extend(items.values())
            tables.append(asked[m][0] if m else request)
        packs = pack(tuple(lists), cap, bases, tables, pieces, after)
        got = [swap(value, m) if m else value for value, (m, *_) in zip(packs, chosen)]
        for value, (m, items, start, count) in zip(got, chosen):
            for c, sub in enumerate(subs):
                if start <= starts[c] and starts[c] + sub <= start + count:
                    for i, (k, other) in enumerate(items):
                        for rank, place in enumerate(places(k, other ^ m)):
                            at = (i * cap + rank) * count + starts[c] - start
                            plans[c].append((place, len(sources[c]), at))
                    sources[c].append(value)
        return got

    near = {(0, 0): raw, (0, 1): beside}
    after = pick([(2, near, 0, width)], [])
    after = after + [design[0], tiles] + [asked[m][0] for m in range(4, group, 4)]
    arrived = {(0, m): value for m, value in across_raw.items()}
    arrived.update({(k, 0): value for k, value in far_raw.items()})
    arrived = {key: follow(value, after) for key, value in arrived.items()}
    second = {(k, m ^ 1): swap(value, 1) for (k, m), value in arrived.items()}
    everything = {**arrived, **second}
    far = {key: value for key, value in everything.items() if key[0]}
    pick([(6, far, 0, width), (4, far, 0, subs[0])], [])
    sooner = pick([(2, arrived, 0, subs[0])], [])
    pick([(2, second, 0, subs[0])], [])
    for start, sub in list(zip(starts, subs))[1:]:
        pick([(2, everything, start, sub), (4, far, start, sub)], sooner)
    pick([(0, {**near, **arrived, **second}, 0, width)], [])
    smoothed = [
        smooth(tuple(plans[c]), table, sources[c], sub, tiles, block_count)
        for c, sub in enumerate(subs)
    ]
    parts = list(smoothed)
    for shift in range(1, subj_count):
        pairs = [(i, (i + shift) % subj_count) for i in range(subj_count)]
        parts.extend(lax.ppermute(value, "subj", pairs) for value in smoothed)
    total = project(design[:-1], parts[:-1], [], False)
    return project(design[-1:], parts[-1:], [total], True)


def solution(mesh):
    placed = (
        P("fix", "subj"),
        P("fix", None, None, None),
        P("fix", None),
        P(None, "subj"),
        P(None, "subj"),
        P(),
        P(None, "subj"),
    )
    return jax.shard_map(
        per_device, mesh=mesh, in_specs=placed, out_specs=P("subj", "fix"), check_vma=False
    )
```

```python
import functools

import jax
import jax.numpy as jnp
import numpy as np
from jax import lax
from jax.experimental import pallas as pl
from jax.experimental.pallas import tpu as pltpu
from jax.sharding import PartitionSpec as P

GROUP = 8
SHARES = (1, 1)
LANES = 128
ANY = pl.BlockSpec(memory_space=pl.ANY)
SMEM = pl.BlockSpec(memory_space=pltpu.SMEM)
VMEM = pl.BlockSpec(memory_space=pltpu.VMEM)
PARAMS = pltpu.CompilerParams(vmem_limit_bytes=16 * 1024 * 1024)


def cost(flops, bytes_accessed):
    return pl.CostEstimate(flops=flops, bytes_accessed=bytes_accessed, transcendentals=0)


def split(value):
    high = value.astype(jnp.bfloat16)
    return high, (value - high.astype(jnp.float32)).astype(jnp.bfloat16)


def follow_kernel(*refs):
    pass


def follow(value, after):
    return pl.pallas_call(
        follow_kernel,
        out_shape=jax.ShapeDtypeStruct(value.shape, value.dtype),
        in_specs=[ANY] * (1 + len(after)),
        out_specs=ANY,
        input_output_aliases={0: 0},
        compiler_params=PARAMS,
        cost_estimate=cost(0, 0),
    )(value, *after)


def copy_kernel(value_ref, *refs):
    refs[-1][...] = value_ref[...]


def follow_copy(value, after):
    return pl.pallas_call(
        copy_kernel,
        out_shape=jax.ShapeDtypeStruct(value.shape, value.dtype),
        in_specs=[VMEM] + [ANY] * len(after),
        out_specs=VMEM,
        compiler_params=PARAMS,
        cost_estimate=cost(0, 8 * value.size),
    )(value, *after)


def tiles_kernel(conn_ref, out_ref):
    size = conn_ref.shape[1]
    for t in range(conn_ref.shape[0]):
        high, low = split(conn_ref[t].T)
        out_ref[t, :, :size] = high
        out_ref[t, :, size:] = low


def split_tiles(conn):
    total, size, _ = conn.shape
    return pl.pallas_call(
        tiles_kernel,
        out_shape=jax.ShapeDtypeStruct((total, size, 2 * size), jnp.bfloat16),
        in_specs=[VMEM],
        out_specs=VMEM,
        compiler_params=PARAMS,
        cost_estimate=cost(4 * total * size * size, 8 * total * size * size),
    )(conn)


def pack_kernel(lists, cap, counts, base_ref, *refs):
    table_count, piece_count = counts
    tables, pieces = refs[:table_count], refs[table_count : table_count + piece_count]
    outs = refs[-len(lists) :]
    for entries, out in zip(lists, outs):
        at = 0
        for piece, table, row, owner, start, sub in entries:
            for rank in range(cap):
                block = pieces[piece][tables[table][row, base_ref[owner] + rank]]
                out[at : at + sub, :] = block.T[start : start + sub, :]
                at += sub


def pack(lists, cap, bases, tables, pieces, after):
    size = pieces[0].shape[1]
    outs = [
        jax.ShapeDtypeStruct(
            (sum(cap * sub for _, _, _, _, _, sub in entries), size), jnp.float32
        )
        for entries in lists
    ]
    return pl.pallas_call(
        functools.partial(pack_kernel, lists, cap, (len(tables), len(pieces))),
        out_shape=outs,
        in_specs=[SMEM] * (1 + len(tables)) + [VMEM] * len(pieces) + [ANY] * len(after),
        out_specs=[VMEM] * len(outs),
        compiler_params=PARAMS,
        cost_estimate=cost(0, 8 * sum(out.size for out in outs)),
    )(bases, *tables, *pieces, *after)


def smooth_kernel(plan, per_row, source_count, table_ref, *refs):
    sources = refs[:source_count]
    tiles_ref, out_ref, highs, lows = refs[source_count:]
    sub, size = highs.shape[1:]
    block_count = out_ref.shape[1] // size
    for place, source, at in plan:
        tile = table_ref[place]
        highs[tile], lows[tile] = split(sources[source][at : at + sub, :])

    for row in range(block_count):
        span = range(row * per_row, (row + 1) * per_row)
        left = jnp.concatenate(
            [
                jnp.concatenate([highs[tile] for tile in span], axis=1),
                jnp.concatenate([lows[tile] for tile in span], axis=1),
            ],
            axis=0,
        )
        right = jnp.concatenate([tiles_ref[tile] for tile in span], axis=0)
        terms = jnp.dot(left, right, preferred_element_type=jnp.float32)
        value = (terms[:sub, :size] + terms[sub:, :size]) + (
            terms[:sub, size:] + terms[sub:, size:]
        )
        out_ref[:, row * size : (row + 1) * size] = value


def smooth(plan, table, sources, sub, tiles, block_count):
    tile_total, size, _ = tiles.shape
    return pl.pallas_call(
        functools.partial(smooth_kernel, plan, tile_total // block_count, len(sources)),
        out_shape=jax.ShapeDtypeStruct((sub, block_count * size), jnp.float32),
        in_specs=[SMEM] + [VMEM] * (len(sources) + 1),
        out_specs=VMEM,
        scratch_shapes=[pltpu.VMEM((tile_total + 1, sub, size), jnp.bfloat16)] * 2,
        compiler_params=PARAMS,
        cost_estimate=cost(
            8 * tile_total * size * size * sub, 4 * tile_total * size * (sub + size)
        ),
    )(table, *sources, tiles)


def design_kernel(cuts, perm_ref, contrast_ref, nuisance_ref, pinv_ref, *refs):
    outs, rows_ref = refs[:-1], refs[-1]
    perms, subjects = perm_ref.shape
    regressors = contrast_ref.shape[0]
    for start in range(0, subjects, LANES):
        want = perm_ref[:, start : start + LANES].astype(jnp.int32)
        lane, part = want % LANES, want // LANES
        for r in range(regressors):
            value = jnp.zeros((perms, LANES), jnp.float32)
            for base in range(0, subjects, LANES):
                table = jnp.broadcast_to(
                    contrast_ref[r : r + 1, base : base + LANES], (perms, LANES)
                )
                found = jnp.take_along_axis(table, lane, axis=1, mode="promise_in_bounds")
                value = jnp.where(part == base // LANES, found, value)
            rows_ref[start // LANES, pl.ds(r, perms, stride=regressors), :] = value
    design = jnp.concatenate([rows_ref[i] for i in range(rows_ref.shape[0])], axis=1)
    result = design
    for n in range(nuisance_ref.shape[0]):
        weight = jnp.sum(design * nuisance_ref[n : n + 1, :], axis=1, keepdims=True)
        result = result - weight * pinv_ref[n : n + 1, :]
    high, low = split(result)
    for (start, sub), out in zip(cuts, outs):
        columns = slice(start, start + sub)
        out[...] = jnp.concatenate(
            [high[:, columns], high[:, columns], low[:, columns], low[:, columns]], axis=1
        )


def reduced_design(perm, contrast, nuisance, pinv, cuts):
    rows = perm.shape[0] * contrast.shape[0]
    subjects = perm.shape[1]
    return pl.pallas_call(
        functools.partial(design_kernel, cuts),
        out_shape=[jax.ShapeDtypeStruct((rows, 4 * sub), jnp.bfloat16) for _, sub in cuts],
        in_specs=[VMEM] * 4,
        out_specs=[VMEM] * len(cuts),
        scratch_shapes=[pltpu.VMEM((subjects // LANES, rows, LANES), jnp.float32)],
        compiler_params=PARAMS,
        cost_estimate=cost(32 * rows * subjects, 8 * rows * subjects),
    )(perm, contrast, nuisance, pinv)


def project_kernel(count, step, last, *refs):
    designs, parts = refs[:count], refs[count : 2 * count]
    before = refs[2 * count : -3] if last else refs[2 * count : -1]
    out_ref = refs[-3] if last else refs[-1]
    fixels = out_ref.shape[1]
    copies = []
    for i, start in enumerate(range(0, fixels, step)):
        span = slice(start, start + step)
        total = before[0][:, span] if before else None
        for design, part in zip(designs, parts):
            high, low = split(part[:, span])
            term = jnp.dot(
                design[...],
                jnp.concatenate([high, low, high, low], axis=0),
                preferred_element_type=jnp.float32,
            )
            total = term if total is None else total + term
        if last:
            held, sems = refs[-2:]
            held[i] = total
            copy = pltpu.make_async_copy(held.at[i], out_ref.at[:, span], sems.at[i])
            copy.start()
            copies.append(copy)
        else:
            out_ref[:, span] = total
    for copy in copies:
        copy.wait()


def project(designs, parts, before, last):
    rows = designs[0].shape[0]
    fixels = parts[0].shape[1]
    step = 256
    steps = fixels // step
    scratch = [pltpu.VMEM((steps, rows, step), jnp.float32), pltpu.SemaphoreType.DMA((steps,))]
    return pl.pallas_call(
        functools.partial(project_kernel, len(parts), step, last),
        out_shape=jax.ShapeDtypeStruct((rows, fixels), jnp.float32),
        in_specs=[VMEM] * (2 * len(parts) + len(before)),
        out_specs=ANY if last else VMEM,
        scratch_shapes=scratch if last else [],
        compiler_params=PARAMS,
        cost_estimate=cost(
            8 * rows * fixels * sum(part.shape[0] for part in parts), 8 * fixels * rows
        ),
    )(*designs, *parts, *before)


def per_device(fixels, conn_tiles, columns, nuisance, nuisance_pinv, contrast, perm_table):
    fix_count = lax.axis_size("fix")
    subj_count = lax.axis_size("subj")
    group = GROUP if fix_count % GROUP == 0 else 1
    lines = fix_count // group
    block_count, per_row = columns.shape
    size = conn_tiles.shape[2]
    width = fixels.shape[1]
    subs = [width * share // sum(SHARES) for share in SHARES]
    starts = [sum(subs[:c]) for c in range(len(subs))]
    tile_total = block_count * per_row
    cap = (tile_total + fix_count - 1) // fix_count
    me = lax.axis_index("fix")
    part = lax.axis_index("subj")

    def swap(value, mask):
        return lax.ppermute(value, "fix", [(i, i ^ mask) for i in range(fix_count)])

    named = columns.T.reshape(-1)
    positions = jnp.arange(tile_total)
    owners, blocks = named // block_count, named % block_count
    earlier = jnp.logical_and(
        owners[:, None] == owners[None, :], positions[:, None] > positions[None, :]
    )
    slots = owners * cap + jnp.sum(earlier.astype(jnp.int32), axis=1)
    order = jnp.arange(fix_count * cap)
    hits = slots == order[:, None]
    request = jnp.sum(jnp.where(hits, blocks, 0), axis=1).reshape(1, -1).astype(jnp.int32)
    line, member = me // group, me % group
    near_first = (line + lines - np.arange(lines)) % lines * group
    bases = ((near_first[:, None] + (member ^ np.arange(group))) * cap).reshape(-1)
    bases = bases.astype(jnp.int32)
    owner = jnp.repeat(bases, cap) + order % cap
    tile = positions % block_count * per_row + positions // block_count
    table = jnp.sum(jnp.where(slots == owner[:, None], tile - tile_total, 0), axis=1)
    table = (table + tile_total).astype(jnp.int32)

    def places(k, other):
        base = (k * group + other) * cap
        return tuple(range(base, base + cap))

    raw = fixels.reshape(block_count, size, width)
    across_raw = {m: swap(raw, m) for m in range(4, group, 4)}
    far_raw = {}
    for k in range(1, lines):
        pairs = [(i, (i + k * group) % fix_count) for i in range(fix_count)]
        far_raw[k] = lax.ppermute(raw, "fix", pairs)
    beside = swap(raw, 1)
    asked = {2: (swap(request, 2), 0)}
    both_requests = jnp.concatenate([request, asked[2][0]])
    for m in range(4, group, 4):
        pair = swap(both_requests, m)
        asked[m], asked[m + 2] = (pair, 0), (pair, 1)

    perm_table = follow_copy(perm_table, [asked[2][0]])
    rows = perm_table.shape[0] // subj_count
    count = nuisance.shape[0]
    shares = []
    for shift in range(subj_count):
        to = (part + shift) % subj_count
        share = jnp.concatenate(
            [
                lax.dynamic_slice_in_dim(perm_table, to * rows, rows, 0).astype(jnp.float32),
                nuisance,
                nuisance_pinv,
            ]
        )
        if shift:
            pairs = [(i, (i + shift) % subj_count) for i in range(subj_count)]
            share = lax.ppermute(share, "subj", pairs)
        shares.append(share)
    shares = jnp.concatenate(shares, axis=1)
    cuts = [
        (shift * width + start, sub)
        for shift in range(subj_count)
        for start, sub in zip(starts, subs)
    ]
    design = reduced_design(
        shares[:rows], contrast, shares[rows : rows + count], shares[rows + count :], cuts
    )

    tiles = split_tiles(conn_tiles.reshape(tile_total, size, size))

    plans, sources = [[] for _ in subs], [[] for _ in subs]

    def pick(chosen, after):
        pieces, tables, lists = [], [], []
        for index, (m, items, start, count) in enumerate(chosen):
            row = asked[m][1] if m else 0
            lists.append(
                tuple(
                    (len(pieces) + i, index, row, key[0] * group + key[1], start, count)
                    for i, key in enumerate(items)
                )
            )
            pieces.extend(items.values())
            tables.append(asked[m][0] if m else request)
        packs = pack(tuple(lists), cap, bases, tables, pieces, after)
        got = [swap(value, m) if m else value for value, (m, *_) in zip(packs, chosen)]
        for value, (m, items, start, count) in zip(got, chosen):
            for c, sub in enumerate(subs):
                if start <= starts[c] and starts[c] + sub <= start + count:
                    for i, (k, other) in enumerate(items):
                        for rank, place in enumerate(places(k, other ^ m)):
                            at = (i * cap + rank) * count + starts[c] - start
                            plans[c].append((place, len(sources[c]), at))
                    sources[c].append(value)
        return got

    near = {(0, 0): raw, (0, 1): beside}
    after = pick([(2, near, 0, width)], [])
    after = after + [design[0], tiles] + [asked[m][0] for m in range(4, group, 4)]
    arrived = {(0, m): value for m, value in across_raw.items()}
    arrived.update({(k, 0): value for k, value in far_raw.items()})
    arrived = {key: follow(value, after) for key, value in arrived.items()}
    second = {(k, m ^ 1): swap(value, 1) for (k, m), value in arrived.items()}
    everything = {**arrived, **second}
    far = {key: value for key, value in everything.items() if key[0]}
    pick([(6, far, 0, width), (4, far, 0, subs[0])], [])
    sooner = pick([(2, arrived, 0, subs[0])], [])
    pick([(2, second, 0, subs[0])], [])
    local = pick([(0, {**near, **arrived, **second}, 0, width)], [])
    for start, sub in list(zip(starts, subs))[1:]:
        pick([(2, everything, start, sub), (4, far, start, sub)], sooner + local)
    smoothed = [
        smooth(tuple(plans[c]), table, sources[c], sub, tiles, block_count)
        for c, sub in enumerate(subs)
    ]
    parts = list(smoothed)
    for shift in range(1, subj_count):
        pairs = [(i, (i + shift) % subj_count) for i in range(subj_count)]
        parts.extend(lax.ppermute(value, "subj", pairs) for value in smoothed)
    total = project(design[:-1], parts[:-1], [], False)
    return project(design[-1:], parts[-1:], [total], True)


def solution(mesh):
    placed = (
        P("fix", "subj"),
        P("fix", None, None, None),
        P("fix", None),
        P(None, "subj"),
        P(None, "subj"),
        P(),
        P(None, "subj"),
    )
    return jax.shard_map(
        per_device, mesh=mesh, in_specs=placed, out_specs=P("subj", "fix"), check_vma=False
    )
```
